32 devices in a mesh: grp: 2 (over core), dev: 16 (over z, y, x).
Axes of the slice: x: 2, y: 2, z: 4, core: 2. Of those that a mesh axis runs over, the one named last changes fastest.
Arguments:
- state: float32 [2, 24, 24, 4096], P(None, None, None, ('grp', 'dev')), may hold values from -6 to 6
- hamiltonian: float32 [24, 24], replicated, may hold values from -1.2 to 1.2
- mode_rates: float32 [96], replicated, may hold values from 0.05 to 2
- ado_modes: int32 [3, 4096], P(None, ('grp', 'dev')), may hold values from 0 to 96
- link_src: int32 [8, 4096], P(None, ('grp', 'dev')), may hold values from 0 to 191, as said below
- link_site: int32 [8, 4096], P(None, ('grp', 'dev')), may hold values from 0 to 23
- link_coef: float32 [4, 8, 4096], P(None, None, ('grp', 'dev')), may hold values from -2.4 to 2.4
- send_ids: int32 [32, 64], P(('grp', 'dev')), may hold values from 0 to 127
- step_units: int32 [], replicated, may hold values from 12 to 16
Outputs:
- new_state: float32 [2, 24, 24, 4096], P(None, None, None, ('grp', 'dev'))
- error_norm: float32 [], replicated
The draws below stay inside these ranges and needn't reach their ends.
Inputs may be any that keep to these rules, and one draw needn't show every extreme that they name: `link_src`: on each device every received position 128 to 191 is named by 1 to 4 couplings of that device's matrices, and some position by exactly 4.
All inputs are finite; a program needn't handle non-finite values.
Results may differ from the reference program's by a relative error of at most 0.0003.
Values sent between devices are 32-bit elements; how exact they have to be, the bound alone decides.
A program may use at most 128 MiB of HBM per device.

```python
import math
import jax
import jax.numpy as jnp
from jax import lax

N = 24
MODES = 96
DEPTH = 3
LINKS = 8
SLOT = 2
USES = 4
ADO_DEV = 128
PEERS = 32
ADOS = 4096
RECV = 64


def draw_link_src(key, part):

    def one_device(device_key):
        key_rank, key_local, key_keep, key_full = jax.random.split(device_key, 4)
        ranking = jax.random.permutation(key_rank, LINKS * ADO_DEV)
        local = jax.random.randint(key_local, (LINKS * ADO_DEV,), 0, ADO_DEV)
        keeping = jax.random.randint(key_keep, (LINKS * ADO_DEV,), 0, 2)
        fullest = jax.random.randint(key_full, (), 0, RECV)
        position = ranking % RECV
        copies = ranking // RECV
        remote = (ranking < RECV * USES) & ((copies == 0) | (keeping == 1) | (position == fullest))
        chosen = jnp.where(remote, ADO_DEV + position, local)
        return chosen.astype(jnp.int32).reshape(LINKS, ADO_DEV)
    blocks = jax.vmap(one_device)(jax.random.split(jax.random.fold_in(key, 7), PEERS))
    return jnp.transpose(blocks, (1, 0, 2)).reshape(LINKS, PEERS * ADO_DEV)


def set_ends(values, stream_key, least, high):
    index_at = [jax.random.randint(jax.random.fold_in(stream_key, axis), (), 0, length) for axis, length in enumerate(values.shape)]
    longest = values.shape.index(max(values.shape))
    neighbour = index_at[:longest] + [(index_at[longest] + 1) % values.shape[longest]] + index_at[longest + 1:]
    return values.at[tuple(index_at)].set(least).at[tuple(neighbour)].set(high)


def shard_levels(key, dims, cuts, smallest, high):
    def one(dim, shards_of):
        draws = jax.random.uniform(jax.random.fold_in(jax.random.fold_in(key, 6), dim), (shards_of,), jnp.float32, smallest / len(cuts), high / len(cuts))
        return jnp.repeat(jnp.exp(draws), dims[dim] // shards_of).reshape((-1,) + (1,) * (len(dims) - dim - 1))

    factor_of = one(*cuts[0])
    for cut in cuts[1:]:
        factor_of = factor_of * one(*cut)
    return factor_of


def normal_values(key, extent, scale, bound, cuts=(), kind=jnp.bfloat16):
    values = scale * jax.random.normal(key, extent, jnp.float32)
    if cuts:
        values = values * shard_levels(key, extent, cuts, -0.22, 0.18)
    return jnp.clip(values, -bound, bound).astype(kind)


def setup_inputs(seed: int = 0) -> dict:
    key_list = jax.random.split(jax.random.key(seed), 10)
    state = normal_values(key_list[0], (2, N, N, ADOS), 1.0, 6.0, ((3, 32),), jnp.float32)
    hamiltonian = normal_values(key_list[1], (N, N), 0.3, 1.2, (), jnp.float32)
    mode_rates = jnp.clip(jnp.exp(jax.random.uniform(key_list[2], (MODES,), jnp.float32, math.log(0.05), math.log(2.0))), 0.05, 2.0)
    ado_modes = set_ends(jax.random.randint(key_list[3], (DEPTH, ADOS), 0, MODES + 1), jax.random.fold_in(key_list[3], 1), 0, MODES).astype(jnp.int32)
    link_src = draw_link_src(jax.random.fold_in(key_list[9], 71), 0)
    link_site = set_ends(jax.random.randint(key_list[5], (LINKS, ADOS), 0, N), jax.random.fold_in(key_list[5], 1), 0, N - 1).astype(jnp.int32)
    link_coef = normal_values(key_list[6], (4, LINKS, ADOS), 0.8, 2.4, ((2, 32),), jnp.float32)
    send_ids = set_ends(jax.random.randint(key_list[7], (PEERS, RECV), 0, ADO_DEV), jax.random.fold_in(key_list[7], 1), 0, ADO_DEV - 1).astype(jnp.int32)
    step_units = jax.random.randint(key_list[8], (), 12, 17).astype(jnp.int32)
    return dict(state=state, hamiltonian=hamiltonian, mode_rates=mode_rates, ado_modes=ado_modes, link_src=link_src, link_site=link_site, link_coef=link_coef, send_ids=send_ids, step_units=step_units)


TABLEAU = ((0.2,), (3.0 / 40, 9.0 / 40), (44.0 / 45, -56.0 / 15, 32.0 / 9), (19372.0 / 6561, -25360.0 / 2187, 64448.0 / 6561, -212.0 / 729), (9017.0 / 3168, -355.0 / 33, 46732.0 / 5247, 49.0 / 176, -5103.0 / 18656), (35.0 / 384, 0.0, 500.0 / 1113, 125.0 / 192, -2187.0 / 6784, 11.0 / 84))
ERRORS = (71.0 / 57600, 0.0, -71.0 / 16695, 71.0 / 1920, -17253.0 / 339200, 22.0 / 525, -1.0 / 40)
ABS_TOL = 0.001
REL_TOL = 0.01
UNIT_STEP = 1.0 / 64

def commute(symmetric, current):
    left_prod = jnp.einsum('ab,sbcx->sacx', symmetric, current, precision=lax.Precision.HIGHEST)
    right_prod = jnp.einsum('sabx,bc->sacx', current, symmetric, precision=lax.Precision.HIGHEST)
    return left_prod - right_prod

def decay_rates(ado_modes, mode_rates):
    extended = jnp.concatenate([mode_rates, jnp.zeros((1,), mode_rates.dtype)])
    levels = jnp.arange(extended.shape[0], dtype=jnp.int32)
    hits = (ado_modes[:, None, :] == levels[None, :, None]).astype(mode_rates.dtype)
    return lax.optimization_barrier(jnp.sum(hits * extended[None, :, None], axis=(0, 1)))

def link_term(source, sites, coef):
    levels = jnp.arange(source.shape[1], dtype=jnp.int32)
    indicator = (levels[:, None] == sites[None, :]).astype(source.dtype)
    row_mask = indicator[:, None, :]
    column_mask = indicator[None, :, :]
    weight_real = coef[0] * row_mask - coef[2] * column_mask
    weight_imag = coef[1] * row_mask - coef[3] * column_mask
    real_part = weight_real * source[0] - weight_imag * source[1]
    imag_part = weight_real * source[1] + weight_imag * source[0]
    return jnp.stack([imag_part, -real_part])

def derivative(current, fetch, symmetric, decay, link_site, link_coef):
    commutator = commute(symmetric, current)
    total = jnp.stack([commutator[1], -commutator[0]]) - decay[None, None, None, :] * current
    for link in range(link_site.shape[0]):
        total = total + link_term(fetch(link), link_site[link], link_coef[:, link])
    return total

def dormand_prince(start, step_size, evaluate):
    sections = [evaluate(start)]
    inner = start
    for weights in TABLEAU:
        inner = start
        for weight, section in zip(weights, sections):
            if weight != 0.0:
                inner = inner + step_size * weight * section
        sections.append(evaluate(inner))
    error = jnp.zeros_like(start)
    for weight, section in zip(ERRORS, sections):
        if weight != 0.0:
            error = error + step_size * weight * section
    scale = ABS_TOL + REL_TOL * jnp.maximum(jnp.abs(start), jnp.abs(inner))
    partial_sum = jnp.sum(jnp.square(error / scale))
    return (inner, partial_sum)

def reference(state, hamiltonian, mode_rates, ado_modes, link_src, link_site, link_coef, send_ids, step_units):
    total_ados = state.shape[3]
    owner = jnp.arange(total_ados, dtype=jnp.int32) // ADO_DEV
    remote = jnp.maximum(link_src - ADO_DEV, 0)
    source_dev = remote // SLOT
    within = remote % SLOT
    column = owner[None, :] * SLOT + within
    sent = send_ids[source_dev, column]
    global_index = jnp.where(link_src < ADO_DEV, owner[None, :] * ADO_DEV + link_src, source_dev * ADO_DEV + sent).astype(jnp.int32)
    symmetric = 0.5 * (hamiltonian + hamiltonian.T)
    decay = decay_rates(ado_modes, mode_rates)
    step_size = step_units.astype(state.dtype) * UNIT_STEP

    def evaluate(current):
        return derivative(current, lambda link: jnp.take(current, global_index[link], axis=3), symmetric, decay, link_site, link_coef)
    new_state, partial_sum = dormand_prince(state, step_size, evaluate)
    entries = 2 * state.shape[1] * state.shape[2] * total_ados
    return (new_state, jnp.sqrt(partial_sum / entries))
```

```python
import functools
from fractions import Fraction as Q

import jax
import jax.numpy as jnp
from jax import lax
from jax.experimental import pallas as pl
from jax.experimental.pallas import tpu as pltpu
from jax.sharding import PartitionSpec as P

TABLEAU = (
    (Q(1, 5),),
    (Q(3, 40), Q(9, 40)),
    (Q(44, 45), Q(-56, 15), Q(32, 9)),
    (Q(19372, 6561), Q(-25360, 2187), Q(64448, 6561), Q(-212, 729)),
    (Q(9017, 3168), Q(-355, 33), Q(46732, 5247), Q(49, 176), Q(-5103, 18656)),
    (Q(35, 384), Q(0), Q(500, 1113), Q(125, 192), Q(-2187, 6784), Q(11, 84)),
)
ERRORS = (Q(71, 57600), Q(0), Q(-71, 16695), Q(71, 1920), Q(-17253, 339200), Q(22, 525), Q(-1, 40))
ABS_TOL = 0.001
REL_TOL = 0.01
UNIT_STEP = 1.0 / 64
USES = 4
HIGHEST = lax.Precision.HIGHEST
MESH = pl.DeviceIdType.MESH
F32 = jnp.float32
BF16 = jnp.bfloat16


def step_polynomials():
    degree = len(ERRORS) + 1

    def combine(weights, sections, constant):
        total = [Q(constant)] + [Q(0)] * (degree - 1)
        for weight, section in zip(weights, sections):
            total = [t + weight * s for t, s in zip(total, section)]
        return total

    def advance(poly):
        return [Q(0)] + poly[:-1]

    sections = [advance(combine((), (), 1))]
    inner = None
    for weights in TABLEAU:
        inner = combine(weights, sections, 1)
        sections.append(advance(inner))
    error = combine(ERRORS, sections, 0)
    return [float(c) for c in inner], [float(c) for c in error]


NEW_POLY, ERR_POLY = step_polynomials()


def one_hot(condition, dtype):
    return jnp.where(condition, 1.0, 0.0).astype(dtype)


def iota(shape, dim):
    return lax.broadcasted_iota(jnp.int32, shape, dim)


def split(values):
    high = values.astype(BF16)
    return high, (values - high.astype(F32)).astype(BF16)


def dot(lhs, rhs):
    return jnp.dot(lhs, rhs, preferred_element_type=F32)


def dot_nt(lhs, rhs, precision=None):
    return lax.dot_general(
        lhs, rhs, (((1,), (1,)), ((), ())), precision=precision, preferred_element_type=F32
    )


def pick_scalar(index, table):
    value = jnp.float32(0.0)
    for place, entry in enumerate(table):
        if entry != 0.0:
            value = jnp.where(index == place, jnp.float32(entry), value)
    return value


def kernel(
    groups,
    members,
    state_ref,
    ham_ref,
    rates_ref,
    modes_ref,
    src_ref,
    site_ref,
    coef_ref,
    ids_ref,
    units_ref,
    out_ref,
    norm_ref,
    w_ref,
    err_ref,
    part_ref,
    super_ref,
    pick_ref,
    select_ref,
    request_ref,
    left_ref,
    right_ref,
    row_ref,
    col_ref,
    asked_row_ref,
    asked_col_ref,
    chosen_ref,
    cols_ref,
    halves_ref,
    fetched_ref,
    tl_ref,
    tr_ref,
    send_ref,
    recv_ref,
    send_sem,
    recv_sem,
):
    peers = groups * members
    sites = state_ref.shape[1]
    owned = state_ref.shape[3]
    links = src_ref.shape[0]
    received = ids_ref.shape[1]
    wide = links * owned
    asks = received * USES
    rows = asks // peers
    pairs = sites * sites
    width = send_ref.shape[1]
    my_grp, my_dev = lax.axis_index("grp"), lax.axis_index("dev")
    me = my_grp * members + my_dev

    def peer_id(step):
        peer = lax.rem(me + step, peers)
        return peer, (peer // members, lax.rem(peer, members))

    barrier = pltpu.get_barrier_semaphore()

    def greet(step, carry):
        _, target = peer_id(step)
        pl.semaphore_signal(barrier, inc=1, device_id=target, device_id_type=MESH)
        return carry

    lax.fori_loop(1, peers, greet, 0)

    def send_all(turn):
        def send(step, carry):
            peer, target = peer_id(step)
            pltpu.make_async_remote_copy(
                src_ref=send_ref.at[pl.ds(pl.multiple_of(peer * rows, rows), rows)],
                dst_ref=recv_ref.at[turn, pl.ds(pl.multiple_of(me * rows, rows), rows)],
                send_sem=send_sem.at[turn],
                recv_sem=recv_sem.at[turn],
                device_id=target,
                device_id_type=MESH,
            ).start()
            return carry

        lax.fori_loop(1, peers, send, 0)
        mine = pl.ds(pl.multiple_of(me * rows, rows), rows)
        recv_ref[turn, mine] = send_ref[mine]

    def bulk(turn, sem):
        every = pl.ds(0, (peers - 1) * rows)
        return pltpu.make_async_copy(send_ref.at[every], recv_ref.at[turn, every], sem.at[turn])

    def wait_all(turn):
        bulk(turn, recv_sem).wait()
        bulk(turn, send_sem).wait()

    step_size = units_ref[0, 0].astype(F32) * UNIT_STEP
    earlier = one_hot(iota((owned, owned), 0) < iota((owned, owned), 1), BF16)
    base = jnp.zeros((received, 1), F32)
    wanted = jnp.zeros((asks, owned), F32)
    for link in range(links):
        lanes = slice(link * owned, (link + 1) * owned)
        source = src_ref[link : link + 1, :]
        site = site_ref[link : link + 1, :]
        hit = iota((received, owned), 0) == source - owned
        hits = one_hot(hit, F32)
        before = dot(one_hot(hit, BF16), earlier) + base
        rank = jnp.sum(hits * before, axis=0, keepdims=True).astype(jnp.int32)
        base = base + jnp.sum(hits, axis=1, keepdims=True)
        ask = jnp.where(source >= owned, (source - owned) * USES + rank, -1)
        asking = iota((asks, owned), 0) == ask
        wanted = wanted + jnp.where(asking, site.astype(F32), 0.0)
        request_ref[:, lanes] = one_hot(asking, BF16)
        local = one_hot(iota((owned, owned), 0) == source, BF16)
        select_ref[:owned, lanes] = local
        select_ref[owned:, lanes] = local
    send_ref[...] = jnp.broadcast_to(jnp.sum(wanted, axis=1, keepdims=True), (asks, width))
    pl.semaphore_wait(barrier, peers - 1)
    send_all(0)

    for link in range(links):
        lanes = slice(link * owned, (link + 1) * owned)
        site = site_ref[link : link + 1, :]
        col_mask = one_hot(iota((sites, owned), 0) == site, F32)
        col_ref[:, lanes] = col_mask
        row_mask = one_hot(iota((sites, 1, owned), 0) == site[None], F32)
        row_ref[:, :, lanes] = row_mask
        for part in range(2):
            left = coef_ref[part, link : link + 1, :] * step_size
            right = coef_ref[part + 2, link : link + 1, :] * step_size
            left_ref[part, :, :, lanes] = row_mask * left[None]
            right_ref[part, :, lanes] = col_mask * right
    flat_coef = [
        jnp.concatenate([coef_ref[k, link : link + 1, :] for link in range(links)], axis=1)
        * step_size
        for k in range(4)
    ]
    first = one_hot(iota((sites, sites, sites), 0) == iota((sites, sites, sites), 2), F32)
    second = one_hot(iota((sites, sites, sites), 1) == iota((sites, sites, sites), 2), F32)
    first, second = first.reshape(pairs, sites), second.reshape(pairs, sites)
    ham = ham_ref[...] * (0.5 * step_size)

    def lifted(hot):
        half = jnp.dot(hot, ham, precision=HIGHEST, preferred_element_type=F32)
        half = half + dot_nt(hot, ham, HIGHEST)
        return dot_nt(half, hot, HIGHEST)

    same_first = dot_nt(first.astype(BF16), first.astype(BF16))
    same_second = dot_nt(second.astype(BF16), second.astype(BF16))
    operator = lifted(first) * same_second - lifted(second) * same_first
    high, low = split(operator)
    super_ref[:pairs] = high
    super_ref[pairs:] = low
    modes = rates_ref.shape[1]
    counts = jnp.zeros((modes, owned), F32)
    for depth in range(modes_ref.shape[0]):
        counts = counts + one_hot(iota((modes, owned), 0) == modes_ref[depth : depth + 1, :], F32)
    rates = jnp.broadcast_to(rates_ref[...], (8, modes))
    decay = jnp.dot(rates, counts, precision=HIGHEST, preferred_element_type=F32)[0:1] * step_size
    spread_low = iota((received, asks), 0) * USES
    spread_at = iota((received, asks), 1)
    spread = one_hot((spread_at >= spread_low) & (spread_at < spread_low + USES), BF16)
    ids = jnp.broadcast_to(ids_ref[...].astype(F32), (16, received)).astype(BF16)
    ids = dot(ids, spread)[0:1].astype(jnp.int32)
    picks = one_hot(iota((owned, asks), 0) == ids, BF16)
    pick_ref[:owned] = picks
    pick_ref[owned:] = picks
    w_ref[...] = state_ref[...]
    out_ref[...] = state_ref[...]
    err_ref[...] = jnp.zeros(err_ref.shape, F32)

    wait_all(0)
    asked = recv_ref[0].T[0:1].astype(jnp.int32)
    asked_col_ref[...] = one_hot(iota((sites, asks), 0) == asked, F32)
    asked_row_ref[...] = one_hot(iota((sites, 1, asks), 0) == asked[None], F32)

    def advance(turn, carry):
        high, low = split(w_ref[...].reshape(2 * pairs, owned))
        halves_ref[...] = jnp.concatenate([high, low], axis=1)
        chosen_ref[...] = dot(halves_ref[...], pick_ref[...]).reshape(2, sites, sites, asks)

        def extract(row, total):
            block = chosen_ref[:, row]
            cols_ref[:, pl.ds(row, 1), :] = jnp.sum(
                block * asked_col_ref[...][None], axis=1, keepdims=True
            )
            return total + block * asked_row_ref[row][None]

        picked = lax.fori_loop(0, sites, extract, jnp.zeros((2, sites, asks), F32))
        outgoing = jnp.concatenate(
            [
                picked.reshape(2 * sites, asks),
                cols_ref[...].reshape(2 * sites, asks),
                jnp.zeros((width - 4 * sites, asks), F32),
            ],
            axis=0,
        )
        send_ref[...] = outgoing.T
        send_all(turn)

        fetched_ref[...] = dot(halves_ref[...], select_ref[...]).reshape(2, sites, sites, wide)
        high = jnp.concatenate([halves_ref[:pairs, :owned], halves_ref[pairs:, :owned]], axis=1)
        low = jnp.concatenate([halves_ref[:pairs, owned:], halves_ref[pairs:, owned:]], axis=1)
        both = dot(super_ref[...], high)
        bracket = both[:pairs] + both[pairs:] + dot(super_ref[:pairs], low)
        part_ref[0] = bracket[:, owned:].reshape(sites, sites, owned) - decay * w_ref[0]
        part_ref[1] = -bracket[:, :owned].reshape(sites, sites, owned) - decay * w_ref[1]

        def near(row, carry):
            real, imag = part_ref[0, row], part_ref[1, row]
            for link in range(links):
                lanes = slice(link * owned, (link + 1) * owned)
                weight_real = left_ref[0, row, :, lanes] - right_ref[0, :, lanes]
                weight_imag = left_ref[1, row, :, lanes] - right_ref[1, :, lanes]
                source_real = fetched_ref[0, row, :, lanes]
                source_imag = fetched_ref[1, row, :, lanes]
                real = real + weight_real * source_imag + weight_imag * source_real
                imag = imag + weight_imag * source_imag - weight_real * source_real
            part_ref[0, row] = real
            part_ref[1, row] = imag
            return carry

        lax.fori_loop(0, sites, near, 0)

        wait_all(turn)
        high, low = split(recv_ref[turn].T)
        found = dot(jnp.concatenate([high, low], axis=0), request_ref[...])
        found = found[:width] + found[width:]
        row_real, row_imag = found[:sites], found[sites : 2 * sites]
        col_real, col_imag = found[2 * sites : 3 * sites], found[3 * sites : 4 * sites]
        left_real, left_imag, right_real, right_imag = flat_coef
        tl_ref[0] = left_real * row_imag + left_imag * row_real
        tl_ref[1] = left_imag * row_imag - left_real * row_real
        tr_ref[0] = -(right_real * col_imag + right_imag * col_real)[:, None, :]
        tr_ref[1] = (right_real * col_real - right_imag * col_imag)[:, None, :]
        new_weight = pick_scalar(turn, NEW_POLY)
        err_weight = pick_scalar(turn, ERR_POLY)

        def far(row, carry):
            for part in range(2):
                value = part_ref[part, row]
                for link in range(links):
                    lanes = slice(link * owned, (link + 1) * owned)
                    value = value + row_ref[row, :, lanes] * tl_ref[part, :, lanes]
                    value = value + col_ref[:, lanes] * tr_ref[part, row, :, lanes]
                w_ref[part, row] = value
                out_ref[part, row] = out_ref[part, row] + new_weight * value
                err_ref[part, row] = err_ref[part, row] + err_weight * value
            return carry

        lax.fori_loop(0, sites, far, 0)
        return carry

    turns = len(ERRORS)
    lax.fori_loop(1, turns + 1, advance, 0)

    scale = ABS_TOL + REL_TOL * jnp.maximum(jnp.abs(state_ref[...]), jnp.abs(out_ref[...]))
    ratio = err_ref[...] / scale
    tile = jnp.sum((ratio * ratio).reshape(2 * pairs // 8, 8, owned), axis=0)
    tile = jnp.sum(tile, axis=0, keepdims=True)
    tile = jnp.sum(tile, axis=1, keepdims=True)
    send_ref[...] = jnp.broadcast_to(tile, (asks, width))
    last = turns + 1
    send_all(last)
    wait_all(last)
    total = jnp.sum(recv_ref[last], axis=0, keepdims=True) * (1.0 / rows)
    entries = 2 * pairs * owned * peers
    norm_ref[...] = jnp.broadcast_to(jnp.sqrt(total[:, :128] / entries), norm_ref.shape)


def shards(
    state, hamiltonian, mode_rates, ado_modes, link_src, link_site, link_coef, send_ids, step_units
):
    groups = lax.axis_size("grp")
    members = lax.axis_size("dev")
    sites, owned = state.shape[1], state.shape[3]
    links = link_src.shape[0]
    received = send_ids.shape[1]
    asks = received * USES
    wide = links * owned
    pairs = sites * sites
    width = -(-4 * sites // 128) * 128
    turns = len(ERRORS) + 2
    vmem = pl.BlockSpec(memory_space=pltpu.VMEM)
    new_state, norm = pl.pallas_call(
        functools.partial(kernel, groups, members),
        out_shape=(
            jax.ShapeDtypeStruct(state.shape, F32),
            jax.ShapeDtypeStruct((8, 128), F32),
        ),
        in_specs=[vmem] * 8 + [pl.BlockSpec(memory_space=pltpu.SMEM)],
        out_specs=(vmem, vmem),
        scratch_shapes=[
            pltpu.VMEM(state.shape, F32),
            pltpu.VMEM(state.shape, F32),
            pltpu.VMEM(state.shape, F32),
            pltpu.VMEM((2 * pairs, pairs), BF16),
            pltpu.VMEM((2 * owned, asks), BF16),
            pltpu.VMEM((2 * owned, wide), BF16),
            pltpu.VMEM((asks, wide), BF16),
            pltpu.VMEM((2, sites, 1, wide), F32),
            pltpu.VMEM((2, sites, wide), F32),
            pltpu.VMEM((sites, 1, wide), F32),
            pltpu.VMEM((sites, wide), F32),
            pltpu.VMEM((sites, 1, asks), F32),
            pltpu.VMEM((sites, asks), F32),
            pltpu.VMEM((2, sites, sites, asks), F32),
            pltpu.VMEM((2, sites, asks), F32),
            pltpu.VMEM((2 * pairs, 2 * owned), BF16),
            pltpu.VMEM((2, sites, sites, wide), F32),
            pltpu.VMEM((2, sites, wide), F32),
            pltpu.VMEM((2, sites, 1, wide), F32),
            pltpu.VMEM((asks, width), F32),
            pltpu.VMEM((turns, asks, width), F32),
            pltpu.SemaphoreType.DMA((turns,)),
            pltpu.SemaphoreType.DMA((turns,)),
        ],
        compiler_params=pltpu.CompilerParams(
            collective_id=0, has_side_effects=True, vmem_limit_bytes=48 * 1024 * 1024
        ),
    )(
        state,
        hamiltonian,
        mode_rates.reshape(1, -1),
        ado_modes,
        link_src,
        link_site,
        link_coef,
        send_ids,
        step_units.reshape(1, 1),
    )
    return new_state, norm[0, 0]


def solution(mesh):
    return jax.shard_map(
        shards,
        mesh=mesh,
        in_specs=(
            P(None, None, None, ("grp", "dev")),
            P(),
            P(),
            P(None, ("grp", "dev")),
            P(None, ("grp", "dev")),
            P(None, ("grp", "dev")),
            P(None, None, ("grp", "dev")),
            P(("grp", "dev"), None),
            P(),
        ),
        out_specs=(P(None, None, None, ("grp", "dev")), P()),
        check_vma=False,
    )
```

```python
import functools
from fractions import Fraction as Q

import jax
import jax.numpy as jnp
from jax import lax
from jax.experimental import pallas as pl
from jax.experimental.pallas import tpu as pltpu
from jax.sharding import PartitionSpec as P

TABLEAU = (
    (Q(1, 5),),
    (Q(3, 40), Q(9, 40)),
    (Q(44, 45), Q(-56, 15), Q(32, 9)),
    (Q(19372, 6561), Q(-25360, 2187), Q(64448, 6561), Q(-212, 729)),
    (Q(9017, 3168), Q(-355, 33), Q(46732, 5247), Q(49, 176), Q(-5103, 18656)),
    (Q(35, 384), Q(0), Q(500, 1113), Q(125, 192), Q(-2187, 6784), Q(11, 84)),
)
ERRORS = (Q(71, 57600), Q(0), Q(-71, 16695), Q(71, 1920), Q(-17253, 339200), Q(22, 525), Q(-1, 40))
ABS_TOL = 0.001
REL_TOL = 0.01
UNIT_STEP = 1.0 / 64
USES = 4
HIGHEST = lax.Precision.HIGHEST
MESH = pl.DeviceIdType.MESH
F32 = jnp.float32
BF16 = jnp.bfloat16


def step_polynomials():
    degree = len(ERRORS) + 1

    def combine(weights, sections, constant):
        total = [Q(constant)] + [Q(0)] * (degree - 1)
        for weight, section in zip(weights, sections):
            total = [t + weight * s for t, s in zip(total, section)]
        return total

    def advance(poly):
        return [Q(0)] + poly[:-1]

    sections = [advance(combine((), (), 1))]
    inner = None
    for weights in TABLEAU:
        inner = combine(weights, sections, 1)
        sections.append(advance(inner))
    error = combine(ERRORS, sections, 0)
    return [float(c) for c in inner], [float(c) for c in error]


NEW_POLY, ERR_POLY = step_polynomials()


def one_hot(condition, dtype):
    return jnp.where(condition, 1.0, 0.0).astype(dtype)


def iota(shape, dim):
    return lax.broadcasted_iota(jnp.int32, shape, dim)


def split(values):
    high = values.astype(BF16)
    return high, (values - high.astype(F32)).astype(BF16)


def dot(lhs, rhs):
    return jnp.dot(lhs, rhs, preferred_element_type=F32)


def dot_nt(lhs, rhs, precision=None):
    return lax.dot_general(
        lhs, rhs, (((1,), (1,)), ((), ())), precision=precision, preferred_element_type=F32
    )


def kernel(
    groups,
    members,
    state_hbm,
    ham_hbm,
    rates_hbm,
    modes_hbm,
    src_hbm,
    site_hbm,
    coef_hbm,
    ids_hbm,
    units_hbm,
    out_ref,
    norm_ref,
    ham_ref,
    rates_ref,
    modes_ref,
    src_ref,
    site_ref,
    coef_ref,
    ids_ref,
    units_ref,
    power_ref,
    part_ref,
    super_ref,
    pick_ref,
    select_ref,
    request_ref,
    place_ref,
    weight_ref,
    own_row_ref,
    own_col_ref,
    asked_row_ref,
    asked_col_ref,
    chosen_ref,
    cols_ref,
    halves_ref,
    fetched_ref,
    tr_ref,
    send_ref,
    recv_ref,
    load_sem,
    send_sem,
    recv_sem,
):
    peers = groups * members
    sites = state_hbm.shape[1]
    owned = state_hbm.shape[3]
    links = src_ref.shape[0]
    received = ids_ref.shape[1]
    wide = links * owned
    asks = received * USES
    rows = asks // peers
    pairs = sites * sites
    width = send_ref.shape[1]
    my_grp, my_dev = lax.axis_index("grp"), lax.axis_index("dev")
    me = my_grp * members + my_dev

    def wrap(value, size):
        return jnp.where(value >= size, value - size, value)

    def each_peer(visit):
        for jump in range(1, groups):
            visit(wrap(my_grp + jump, groups), my_dev)

        def ring(step, carry):
            dev = wrap(my_dev + step, members)
            for jump in range(groups):
                visit(wrap(my_grp + jump, groups), dev)
            return carry

        lax.fori_loop(1, members, ring, 0)

    barrier = pltpu.get_barrier_semaphore()

    def greet(grp, dev):
        pl.semaphore_signal(barrier, inc=1, device_id=(grp, dev), device_id_type=MESH)

    loads = [
        pltpu.make_async_copy(source, target, load_sem.at[place])
        for place, (source, target) in enumerate(
            (
                (src_hbm, src_ref),
                (site_hbm, site_ref),
                (coef_hbm, coef_ref),
                (units_hbm, units_ref),
                (ham_hbm, ham_ref),
                (rates_hbm, rates_ref),
                (modes_hbm, modes_ref),
                (ids_hbm, ids_ref),
                (state_hbm, power_ref.at[0]),
            )
        )
    ]
    for load in loads:
        load.start()
    each_peer(greet)

    def send_all(turn):
        mine = pl.ds(pl.multiple_of(me * rows, rows), rows)

        def send(grp, dev):
            peer = grp * members + dev
            pltpu.make_async_remote_copy(
                src_ref=send_ref.at[pl.ds(pl.multiple_of(peer * rows, rows), rows)],
                dst_ref=recv_ref.at[turn, mine],
                send_sem=send_sem.at[turn],
                recv_sem=recv_sem.at[turn],
                device_id=(grp, dev),
                device_id_type=MESH,
            ).start()

        each_peer(send)
        recv_ref[turn, mine] = send_ref[mine]

    def bulk(turn, sem):
        every = pl.ds(0, (peers - 1) * rows)
        return pltpu.make_async_copy(send_ref.at[every], recv_ref.at[turn, every], sem.at[turn])

    def wait_all(turn):
        bulk(turn, recv_sem).wait()
        bulk(turn, send_sem).wait()

    earlier = one_hot(iota((owned, owned), 0) < iota((owned, owned), 1), BF16)
    base = jnp.zeros((received, 1), F32)
    wanted = jnp.zeros((asks, owned), F32)
    place = jnp.zeros((asks, owned), F32)
    loads[0].wait()
    loads[1].wait()
    for link in range(links):
        lanes = slice(link * owned, (link + 1) * owned)
        source = src_ref[link : link + 1, :]
        site = site_ref[link : link + 1, :]
        hit = iota((received, owned), 0) == source - owned
        hits = one_hot(hit, F32)
        before = dot(one_hot(hit, BF16), earlier) + base
        rank = jnp.sum(hits * before, axis=0, keepdims=True).astype(jnp.int32)
        base = base + jnp.sum(hits, axis=1, keepdims=True)
        ask = jnp.where(source >= owned, (source - owned) * USES + rank, -1)
        asking = iota((asks, owned), 0) == ask
        wanted = wanted + jnp.where(asking, site.astype(F32), 0.0)
        request = one_hot(asking, F32)
        request_ref[:, lanes] = request
        place = place + request
        local = one_hot(iota((owned, owned), 0) == source, BF16)
        select_ref[:owned, lanes] = local
        select_ref[owned:, lanes] = local
    send_ref[...] = jnp.broadcast_to(jnp.sum(wanted, axis=1, keepdims=True), (asks, width))
    pl.semaphore_wait(barrier, peers - 1)
    send_all(0)

    place_ref[:asks] = place.astype(BF16)
    place_ref[asks:] = place.astype(BF16)
    for load in loads[2:]:
        load.wait()
    step_size = units_ref[0, 0].astype(F32) * UNIT_STEP

    def flat(ref):
        return jnp.concatenate([ref[link : link + 1, :] for link in range(links)], axis=1)

    table = [flat(coef_ref.at[k]) * step_size for k in range(4)]
    table = table + [flat(site_ref).astype(F32), jnp.zeros((3, wide), F32)]
    table = dot_nt(jnp.concatenate(table, axis=0), request_ref[...], HIGHEST)
    left_real, left_imag = table[0:1], table[1:2]
    right_real, right_imag = table[2:3], table[3:4]
    own_site = jnp.round(table[4:5]).astype(jnp.int32)
    own_col_ref[...] = one_hot(iota((sites, asks), 0) == own_site, F32)
    own_row_ref[...] = one_hot(iota((sites, 1, asks), 0) == own_site[None], F32)
    for link in range(links):
        lanes = slice(link * owned, (link + 1) * owned)
        site = site_ref[link : link + 1, :]
        for part in range(2):
            left = coef_ref[part, link : link + 1, :] * step_size
            right = coef_ref[part + 2, link : link + 1, :] * step_size
            right = jnp.where(iota((sites, owned), 0) == site, right, 0.0)
            for row in range(sites):
                weight_ref[part, row, :, lanes] = jnp.where(site == row, left, 0.0) - right
    first = one_hot(iota((sites, sites, sites), 0) == iota((sites, sites, sites), 2), F32)
    second = one_hot(iota((sites, sites, sites), 1) == iota((sites, sites, sites), 2), F32)
    first, second = first.reshape(pairs, sites), second.reshape(pairs, sites)
    ham = ham_ref[...] * (0.5 * step_size)

    def lifted(hot):
        half = jnp.dot(hot, ham, precision=HIGHEST, preferred_element_type=F32)
        half = half + dot_nt(hot, ham, HIGHEST)
        return dot_nt(half, hot, HIGHEST)

    same_first = dot_nt(first.astype(BF16), first.astype(BF16))
    same_second = dot_nt(second.astype(BF16), second.astype(BF16))
    operator = lifted(first) * same_second - lifted(second) * same_first
    high, low = split(operator)
    super_ref[:pairs] = high
    super_ref[pairs:] = low
    modes = rates_ref.shape[1]
    counts = jnp.zeros((modes, owned), F32)
    for depth in range(modes_ref.shape[0]):
        counts = counts + one_hot(iota((modes, owned), 0) == modes_ref[depth : depth + 1, :], F32)
    rates = jnp.broadcast_to(rates_ref[...], (8, modes))
    decay = jnp.dot(rates, counts, precision=HIGHEST, preferred_element_type=F32)[0:1] * step_size
    spread_low = iota((received, asks), 0) * USES
    spread_at = iota((received, asks), 1)
    spread = one_hot((spread_at >= spread_low) & (spread_at < spread_low + USES), BF16)
    ids = jnp.broadcast_to(ids_ref[...].astype(F32), (16, received)).astype(BF16)
    ids = dot(ids, spread)[0:1].astype(jnp.int32)
    picks = one_hot(iota((owned, asks), 0) == ids, BF16)
    pick_ref[:owned] = picks
    pick_ref[owned:] = picks

    wait_all(0)
    asked = recv_ref[0].T[0:1].astype(jnp.int32)
    asked_col_ref[...] = one_hot(iota((sites, asks), 0) == asked, F32)
    asked_row_ref[...] = one_hot(iota((sites, 1, asks), 0) == asked[None], F32)

    def advance(turn, carry):
        before = turn - 1
        high, low = split(power_ref[before].reshape(2 * pairs, owned))
        halves_ref[...] = jnp.concatenate([high, low], axis=1)
        chosen_ref[...] = dot(halves_ref[...], pick_ref[...]).reshape(2, sites, sites, asks)
        col_mask = asked_col_ref[...]
        picked = []
        for part in range(2):
            total = jnp.zeros((sites, asks), F32)
            for row in range(sites):
                block = chosen_ref[part, row]
                total = total + block * asked_row_ref[row]
                cols_ref[part, row : row + 1, :] = jnp.sum(block * col_mask, axis=0, keepdims=True)
            picked.append(total)
        outgoing = jnp.concatenate(
            picked
            + [cols_ref[...].reshape(2 * sites, asks), jnp.zeros((width - 4 * sites, asks), F32)],
            axis=0,
        )
        send_ref[...] = outgoing.T
        send_all(turn)

        fetched_ref[...] = dot(halves_ref[...], select_ref[...]).reshape(2, sites, sites, wide)
        high = jnp.concatenate([halves_ref[:pairs, :owned], halves_ref[pairs:, :owned]], axis=1)
        low = jnp.concatenate([halves_ref[:pairs, owned:], halves_ref[pairs:, owned:]], axis=1)
        both = dot(super_ref[...], high)
        bracket = both[:pairs] + both[pairs:] + dot(super_ref[:pairs], low)
        part_ref[0] = (
            bracket[:, owned:].reshape(sites, sites, owned) - decay * power_ref[before, 0]
        )
        part_ref[1] = (
            -bracket[:, :owned].reshape(sites, sites, owned) - decay * power_ref[before, 1]
        )

        def near(row, carry):
            real, imag = part_ref[0, row], part_ref[1, row]
            for link in range(links):
                lanes = slice(link * owned, (link + 1) * owned)
                weight_real, weight_imag = (weight_ref[k, row, :, lanes] for k in range(2))
                source_real, source_imag = (fetched_ref[k, row, :, lanes] for k in range(2))
                real = real + (weight_real * source_imag + weight_imag * source_real)
                imag = imag + (weight_imag * source_imag - weight_real * source_real)
            part_ref[0, row] = real
            part_ref[1, row] = imag
            return carry

        lax.fori_loop(0, sites, near, 0)

        wait_all(turn)
        found = recv_ref[turn].T
        row_real, row_imag = found[:sites], found[sites : 2 * sites]
        col_real, col_imag = found[2 * sites : 3 * sites], found[3 * sites : 4 * sites]
        tl = (
            left_real * row_imag + left_imag * row_real,
            left_imag * row_imag - left_real * row_real,
        )
        tr_ref[0] = -(right_real * col_imag + right_imag * col_real)
        tr_ref[1] = right_real * col_real - right_imag * col_imag
        own_col = own_col_ref[...]
        blocks = [
            tl[part] * own_row_ref[row] + own_col * tr_ref[part, row : row + 1, :]
            for part in range(2)
            for row in range(sites)
        ]
        high, low = split(jnp.concatenate(blocks, axis=0))
        far = dot(jnp.concatenate([high, low], axis=1), place_ref[...])
        power_ref[turn] = part_ref[...] + far.reshape(2, sites, sites, owned)
        return carry

    turns = len(ERRORS)
    lax.fori_loop(1, turns + 1, advance, 0)

    def combine(poly):
        terms = [
            power_ref[k] if c == 1.0 else power_ref[k] * c for k, c in enumerate(poly) if c != 0.0
        ]
        return functools.reduce(jnp.add, terms)

    out_ref[...] = combine(NEW_POLY)
    scale = ABS_TOL + REL_TOL * jnp.maximum(jnp.abs(power_ref[0]), jnp.abs(out_ref[...]))
    ratio = combine(ERR_POLY) / scale
    tile = jnp.sum((ratio * ratio).reshape(2 * pairs // 8, 8, owned), axis=0)
    tile = jnp.sum(tile, axis=0, keepdims=True)
    tile = jnp.sum(tile, axis=1, keepdims=True)
    send_ref[...] = jnp.broadcast_to(tile, (asks, width))
    last = turns + 1
    send_all(last)
    wait_all(last)
    total = jnp.sum(recv_ref[last], axis=0, keepdims=True) * (1.0 / rows)
    entries = 2 * pairs * owned * peers
    norm_ref[...] = jnp.sqrt(total[:, :1] / entries)


def shards(
    state, hamiltonian, mode_rates, ado_modes, link_src, link_site, link_coef, send_ids, step_units
):
    groups = lax.axis_size("grp")
    members = lax.axis_size("dev")
    sites, owned = state.shape[1], state.shape[3]
    links = link_src.shape[0]
    received = send_ids.shape[1]
    asks = received * USES
    wide = links * owned
    pairs = sites * sites
    width = -(-4 * sites // 128) * 128
    turns = len(ERRORS) + 2
    vmem = pl.BlockSpec(memory_space=pltpu.VMEM)
    hbm = pl.BlockSpec(memory_space=pltpu.HBM)
    new_state, norm = pl.pallas_call(
        functools.partial(kernel, groups, members),
        out_shape=(
            jax.ShapeDtypeStruct(state.shape, F32),
            jax.ShapeDtypeStruct((1, 1), F32),
        ),
        in_specs=[hbm] * 9,
        out_specs=(vmem, vmem),
        scratch_shapes=[
            pltpu.VMEM(hamiltonian.shape, F32),
            pltpu.VMEM((1, mode_rates.shape[0]), F32),
            pltpu.VMEM(ado_modes.shape, jnp.int32),
            pltpu.VMEM(link_src.shape, jnp.int32),
            pltpu.VMEM(link_site.shape, jnp.int32),
            pltpu.VMEM(link_coef.shape, F32),
            pltpu.VMEM(send_ids.shape, jnp.int32),
            pltpu.SMEM((1, 1), jnp.int32),
            pltpu.VMEM((len(ERRORS) + 1,) + state.shape, F32),
            pltpu.VMEM(state.shape, F32),
            pltpu.VMEM((2 * pairs, pairs), BF16),
            pltpu.VMEM((2 * owned, asks), BF16),
            pltpu.VMEM((2 * owned, wide), BF16),
            pltpu.VMEM((asks, wide), F32),
            pltpu.VMEM((2 * asks, owned), BF16),
            pltpu.VMEM((2, sites, sites, wide), F32),
            pltpu.VMEM((sites, 1, asks), F32),
            pltpu.VMEM((sites, asks), F32),
            pltpu.VMEM((sites, 1, asks), F32),
            pltpu.VMEM((sites, asks), F32),
            pltpu.VMEM((2, sites, sites, asks), F32),
            pltpu.VMEM((2, sites, asks), F32),
            pltpu.VMEM((2 * pairs, 2 * owned), BF16),
            pltpu.VMEM((2, sites, sites, wide), F32),
            pltpu.VMEM((2, sites, asks), F32),
            pltpu.VMEM((asks, width), F32),
            pltpu.VMEM((turns, asks, width), F32),
            pltpu.SemaphoreType.DMA((9,)),
            pltpu.SemaphoreType.DMA((turns,)),
            pltpu.SemaphoreType.DMA((turns,)),
        ],
        compiler_params=pltpu.CompilerParams(
            collective_id=0, has_side_effects=True, vmem_limit_bytes=64 * 1024 * 1024
        ),
    )(
        state,
        hamiltonian,
        mode_rates.reshape(1, -1),
        ado_modes,
        link_src,
        link_site,
        link_coef,
        send_ids,
        step_units.reshape(1, 1),
    )
    return new_state, norm.reshape(())


def solution(mesh):
    return jax.shard_map(
        shards,
        mesh=mesh,
        in_specs=(
            P(None, None, None, ("grp", "dev")),
            P(),
            P(),
            P(None, ("grp", "dev")),
            P(None, ("grp", "dev")),
            P(None, ("grp", "dev")),
            P(None, None, ("grp", "dev")),
            P(("grp", "dev"), None),
            P(),
        ),
        out_specs=(P(None, None, None, ("grp", "dev")), P()),
        check_vma=False,
    )
```

```python
import functools
from fractions import Fraction as Q

import jax
import jax.numpy as jnp
from jax import lax
from jax.experimental import pallas as pl
from jax.experimental.pallas import tpu as pltpu
from jax.sharding import PartitionSpec as P

TABLEAU = (
    (Q(1, 5),),
    (Q(3, 40), Q(9, 40)),
    (Q(44, 45), Q(-56, 15), Q(32, 9)),
    (Q(19372, 6561), Q(-25360, 2187), Q(64448, 6561), Q(-212, 729)),
    (Q(9017, 3168), Q(-355, 33), Q(46732, 5247), Q(49, 176), Q(-5103, 18656)),
    (Q(35, 384), Q(0), Q(500, 1113), Q(125, 192), Q(-2187, 6784), Q(11, 84)),
)
ERRORS = (Q(71, 57600), Q(0), Q(-71, 16695), Q(71, 1920), Q(-17253, 339200), Q(22, 525), Q(-1, 40))
ABS_TOL = 0.001
REL_TOL = 0.01
UNIT_STEP = 1.0 / 64
USES = 4
HIGHEST = lax.Precision.HIGHEST
MESH = pl.DeviceIdType.MESH
F32 = jnp.float32
BF16 = jnp.bfloat16


def step_polynomials():
    degree = len(ERRORS) + 1

    def combine(weights, sections, constant):
        total = [Q(constant)] + [Q(0)] * (degree - 1)
        for weight, section in zip(weights, sections):
            total = [t + weight * s for t, s in zip(total, section)]
        return total

    def advance(poly):
        return [Q(0)] + poly[:-1]

    sections = [advance(combine((), (), 1))]
    inner = None
    for weights in TABLEAU:
        inner = combine(weights, sections, 1)
        sections.append(advance(inner))
    error = combine(ERRORS, sections, 0)
    return [float(c) for c in inner], [float(c) for c in error]


NEW_POLY, ERR_POLY = step_polynomials()


def one_hot(condition, dtype):
    return jnp.where(condition, 1.0, 0.0).astype(dtype)


def iota(shape, dim):
    return lax.broadcasted_iota(jnp.int32, shape, dim)


def split(values):
    high = values.astype(BF16)
    return high, (values - high.astype(F32)).astype(BF16)


def dot(lhs, rhs):
    return jnp.dot(lhs, rhs, preferred_element_type=F32)


def dot_nt(lhs, rhs, precision=None):
    return lax.dot_general(
        lhs, rhs, (((1,), (1,)), ((), ())), precision=precision, preferred_element_type=F32
    )


def kernel(
    groups,
    members,
    state_hbm,
    ham_hbm,
    rates_hbm,
    modes_hbm,
    src_hbm,
    site_hbm,
    coef_hbm,
    ids_hbm,
    units_hbm,
    out_ref,
    norm_ref,
    ham_ref,
    rates_ref,
    modes_ref,
    src_ref,
    site_ref,
    coef_ref,
    ids_ref,
    units_ref,
    power_ref,
    part_ref,
    super_ref,
    pick_ref,
    select_ref,
    request_ref,
    place_ref,
    weight_ref,
    own_row_ref,
    own_col_ref,
    asked_row_ref,
    asked_col_ref,
    chosen_ref,
    cols_ref,
    halves_ref,
    fetched_ref,
    tr_ref,
    send_ref,
    recv_ref,
    note_ref,
    noted_ref,
    load_sem,
    send_sem,
    recv_sem,
    note_send_sem,
    note_recv_sem,
):
    peers = groups * members
    sites = state_hbm.shape[1]
    owned = state_hbm.shape[3]
    links = src_ref.shape[0]
    received = ids_ref.shape[1]
    wide = links * owned
    asks = received * USES
    rows = asks // peers
    pairs = sites * sites
    width = send_ref.shape[1]
    my_grp, my_dev = lax.axis_index("grp"), lax.axis_index("dev")
    me = my_grp * members + my_dev

    def wrap(value, size):
        return jnp.where(value >= size, value - size, value)

    def each_peer(visit, unroll=False):
        for jump in range(1, groups):
            visit(wrap(my_grp + jump, groups), my_dev)

        def ring(step, carry):
            dev = wrap(my_dev + step, members)
            for jump in range(groups):
                visit(wrap(my_grp + jump, groups), dev)
            return carry

        if unroll:
            for step in range(1, members):
                ring(step, 0)
        else:
            lax.fori_loop(1, members, ring, 0)

    barrier = pltpu.get_barrier_semaphore()

    def greet(grp, dev):
        pl.semaphore_signal(barrier, inc=1, device_id=(grp, dev), device_id_type=MESH)

    loads = [
        pltpu.make_async_copy(source, target, load_sem.at[place])
        for place, (source, target) in enumerate(
            (
                (src_hbm, src_ref),
                (site_hbm, site_ref),
                (coef_hbm, coef_ref),
                (units_hbm, units_ref),
                (ham_hbm, ham_ref),
                (rates_hbm, rates_ref),
                (modes_hbm, modes_ref),
                (ids_hbm, ids_ref),
                (state_hbm, power_ref.at[0]),
            )
        )
    ]
    for load in loads:
        load.start()
    each_peer(greet)

    def send_all(turn):
        mine = pl.ds(pl.multiple_of(me * rows, rows), rows)

        def send(grp, dev):
            peer = grp * members + dev
            pltpu.make_async_remote_copy(
                src_ref=send_ref.at[pl.ds(pl.multiple_of(peer * rows, rows), rows)],
                dst_ref=recv_ref.at[turn - 1, mine],
                send_sem=send_sem.at[turn - 1],
                recv_sem=recv_sem.at[turn - 1],
                device_id=(grp, dev),
                device_id_type=MESH,
            ).start()

        each_peer(send, unroll=True)
        recv_ref[turn - 1, mine] = send_ref[mine]

    def bulk(turn, sem):
        every = pl.ds(0, (peers - 1) * rows)
        return pltpu.make_async_copy(send_ref.at[every], recv_ref.at[turn, every], sem.at[turn])

    def wait_all(turn):
        bulk(turn - 1, recv_sem).wait()
        bulk(turn - 1, send_sem).wait()

    def send_note(note):
        def send(grp, dev):
            pltpu.make_async_remote_copy(
                src_ref=note_ref.at[note, grp * members + dev],
                dst_ref=noted_ref.at[note, me],
                send_sem=note_send_sem.at[note],
                recv_sem=note_recv_sem.at[note],
                device_id=(grp, dev),
                device_id_type=MESH,
            ).start()

        each_peer(send)
        noted_ref[note, me] = note_ref[note, me]

    def wait_note(note):
        every = pl.ds(0, peers - 1)
        for sem in (note_recv_sem, note_send_sem):
            pltpu.make_async_copy(
                note_ref.at[note, every], noted_ref.at[note, every], sem.at[note]
            ).wait()

    earlier = one_hot(iota((owned, owned), 0) < iota((owned, owned), 1), BF16)
    base = jnp.zeros((received, 1), F32)
    wanted = jnp.zeros((asks, owned), F32)
    place = jnp.zeros((asks, owned), F32)
    loads[0].wait()
    loads[1].wait()
    for link in range(links):
        lanes = slice(link * owned, (link + 1) * owned)
        source = src_ref[link : link + 1, :]
        site = site_ref[link : link + 1, :]
        hit = iota((received, owned), 0) == source - owned
        hits = one_hot(hit, F32)
        before = dot(one_hot(hit, BF16), earlier) + base
        rank = jnp.sum(hits * before, axis=0, keepdims=True).astype(jnp.int32)
        base = base + jnp.sum(hits, axis=1, keepdims=True)
        ask = jnp.where(source >= owned, (source - owned) * USES + rank, -1)
        asking = iota((asks, owned), 0) == ask
        wanted = wanted + jnp.where(asking, site.astype(F32), 0.0)
        request = one_hot(asking, F32)
        request_ref[:, lanes] = request
        place = place + request
        local = one_hot(iota((owned, owned), 0) == source, BF16)
        select_ref[:owned, lanes] = local
        select_ref[owned:, lanes] = local
    lane_of = iota((peers, rows, 128), 1) == iota((peers, rows, 128), 2)
    lane_of = one_hot(lane_of, F32).reshape(asks, 128)
    peer_of = iota((peers, rows, peers), 0) == iota((peers, rows, peers), 2)
    peer_of = one_hot(peer_of, F32).reshape(asks, peers)
    wanted = jnp.sum(wanted, axis=1, keepdims=True) * lane_of
    wanted = wanted.reshape(peers, rows, 128).sum(axis=1, keepdims=True)
    note_ref[0] = wanted
    pl.semaphore_wait(barrier, peers - 1)
    send_note(0)

    place_ref[:asks] = place.astype(BF16)
    place_ref[asks:] = place.astype(BF16)
    for load in loads[2:]:
        load.wait()
    step_size = units_ref[0, 0].astype(F32) * UNIT_STEP

    def flat(ref):
        return jnp.concatenate([ref[link : link + 1, :] for link in range(links)], axis=1)

    table = [flat(coef_ref.at[k]) * step_size for k in range(4)]
    table = table + [flat(site_ref).astype(F32), jnp.zeros((3, wide), F32)]
    table = dot_nt(jnp.concatenate(table, axis=0), request_ref[...], HIGHEST)
    left_real, left_imag = table[0:1], table[1:2]
    right_real, right_imag = table[2:3], table[3:4]
    own_site = jnp.round(table[4:5]).astype(jnp.int32)
    own_col_ref[...] = one_hot(iota((sites, asks), 0) == own_site, F32)
    own_row_ref[...] = one_hot(iota((sites, 1, asks), 0) == own_site[None], F32)
    for link in range(links):
        lanes = slice(link * owned, (link + 1) * owned)
        site = site_ref[link : link + 1, :]
        for part in range(2):
            left = coef_ref[part, link : link + 1, :] * step_size
            right = coef_ref[part + 2, link : link + 1, :] * step_size
            right = jnp.where(iota((sites, owned), 0) == site, right, 0.0)
            for row in range(sites):
                weight_ref[part, row, :, lanes] = jnp.where(site == row, left, 0.0) - right
    first = one_hot(iota((sites, sites, sites), 0) == iota((sites, sites, sites), 2), F32)
    second = one_hot(iota((sites, sites, sites), 1) == iota((sites, sites, sites), 2), F32)
    first, second = first.reshape(pairs, sites), second.reshape(pairs, sites)
    ham = ham_ref[...] * (0.5 * step_size)

    def lifted(hot):
        half = jnp.dot(hot, ham, precision=HIGHEST, preferred_element_type=F32)
        half = half + dot_nt(hot, ham, HIGHEST)
        return dot_nt(half, hot, HIGHEST)

    same_first = dot_nt(first.astype(BF16), first.astype(BF16))
    same_second = dot_nt(second.astype(BF16), second.astype(BF16))
    operator = lifted(first) * same_second - lifted(second) * same_first
    high, low = split(operator)
    super_ref[:pairs] = high
    super_ref[pairs:] = low
    modes = rates_ref.shape[1]
    counts = jnp.zeros((modes, owned), F32)
    for depth in range(modes_ref.shape[0]):
        counts = counts + one_hot(iota((modes, owned), 0) == modes_ref[depth : depth + 1, :], F32)
    rates = jnp.broadcast_to(rates_ref[...], (8, modes))
    decay = jnp.dot(rates, counts, precision=HIGHEST, preferred_element_type=F32)[0:1] * step_size
    spread_low = iota((received, asks), 0) * USES
    spread_at = iota((received, asks), 1)
    spread = one_hot((spread_at >= spread_low) & (spread_at < spread_low + USES), BF16)
    ids = jnp.broadcast_to(ids_ref[...].astype(F32), (16, received)).astype(BF16)
    ids = dot(ids, spread)[0:1].astype(jnp.int32)
    picks = one_hot(iota((owned, asks), 0) == ids, BF16)
    pick_ref[:owned] = picks
    pick_ref[owned:] = picks

    wait_note(0)
    asked = dot(peer_of.astype(BF16), noted_ref[0].reshape(peers, 128).astype(BF16))
    asked = jnp.broadcast_to(jnp.sum(asked * lane_of, axis=1, keepdims=True), (asks, 128))
    asked = asked.T[0:1].astype(jnp.int32)
    asked_col_ref[...] = one_hot(iota((sites, asks), 0) == asked, F32)
    asked_row_ref[...] = one_hot(iota((sites, 1, asks), 0) == asked[None], F32)

    def advance(turn, carry):
        before = turn - 1
        high, low = split(power_ref[before].reshape(2 * pairs, owned))
        halves_ref[...] = jnp.concatenate([high, low], axis=1)
        chosen_ref[...] = dot(halves_ref[...], pick_ref[...]).reshape(2, sites, sites, asks)
        col_mask = asked_col_ref[...]
        picked = []
        for part in range(2):
            total = jnp.zeros((sites, asks), F32)
            for row in range(sites):
                block = chosen_ref[part, row]
                total = total + block * asked_row_ref[row]
                cols_ref[part, row : row + 1, :] = jnp.sum(block * col_mask, axis=0, keepdims=True)
            picked.append(total)
        outgoing = jnp.concatenate(
            picked
            + [cols_ref[...].reshape(2 * sites, asks), jnp.zeros((width - 4 * sites, asks), F32)],
            axis=0,
        )
        send_ref[...] = outgoing.T
        send_all(turn)

        fetched_ref[...] = dot(halves_ref[...], select_ref[...]).reshape(2, sites, sites, wide)
        high = jnp.concatenate([halves_ref[:pairs, :owned], halves_ref[pairs:, :owned]], axis=1)
        low = jnp.concatenate([halves_ref[:pairs, owned:], halves_ref[pairs:, owned:]], axis=1)
        both = dot(super_ref[...], high)
        bracket = both[:pairs] + both[pairs:] + dot(super_ref[:pairs], low)
        part_ref[0] = (
            bracket[:, owned:].reshape(sites, sites, owned) - decay * power_ref[before, 0]
        )
        part_ref[1] = (
            -bracket[:, :owned].reshape(sites, sites, owned) - decay * power_ref[before, 1]
        )

        def near(row, carry):
            real, imag = part_ref[0, row], part_ref[1, row]
            for link in range(links):
                lanes = slice(link * owned, (link + 1) * owned)
                weight_real, weight_imag = (weight_ref[k, row, :, lanes] for k in range(2))
                source_real, source_imag = (fetched_ref[k, row, :, lanes] for k in range(2))
                real = real + (weight_real * source_imag + weight_imag * source_real)
                imag = imag + (weight_imag * source_imag - weight_real * source_real)
            part_ref[0, row] = real
            part_ref[1, row] = imag
            return carry

        lax.fori_loop(0, sites, near, 0)

        wait_all(turn)
        found = recv_ref[turn - 1].T
        row_real, row_imag = found[:sites], found[sites : 2 * sites]
        col_real, col_imag = found[2 * sites : 3 * sites], found[3 * sites : 4 * sites]
        tl = (
            left_real * row_imag + left_imag * row_real,
            left_imag * row_imag - left_real * row_real,
        )
        tr_ref[0] = -(right_real * col_imag + right_imag * col_real)
        tr_ref[1] = right_real * col_real - right_imag * col_imag
        own_col = own_col_ref[...]
        blocks = [
            tl[part] * own_row_ref[row] + own_col * tr_ref[part, row : row + 1, :]
            for part in range(2)
            for row in range(sites)
        ]
        high, low = split(jnp.concatenate(blocks, axis=0))
        far = dot(jnp.concatenate([high, low], axis=1), place_ref[...])
        power_ref[turn] = part_ref[...] + far.reshape(2, sites, sites, owned)
        return carry

    turns = len(ERRORS)
    lax.fori_loop(1, turns + 1, advance, 0)

    def combine(poly):
        terms = [
            power_ref[k] if c == 1.0 else power_ref[k] * c for k, c in enumerate(poly) if c != 0.0
        ]
        return functools.reduce(jnp.add, terms)

    increment = combine([0.0] + NEW_POLY[1:])
    out_ref[...] = increment
    new_state = power_ref[0] + increment
    scale = ABS_TOL + REL_TOL * jnp.maximum(jnp.abs(power_ref[0]), jnp.abs(new_state))
    ratio = combine(ERR_POLY) / scale
    tile = jnp.sum((ratio * ratio).reshape(2 * pairs // 8, 8, owned), axis=0)
    tile = jnp.sum(tile, axis=0, keepdims=True)
    tile = jnp.sum(tile, axis=1, keepdims=True)
    note_ref[1] = jnp.broadcast_to(tile[None], (peers, 1, 128))
    send_note(1)
    wait_note(1)
    total = jnp.sum(noted_ref[1], axis=0)
    entries = 2 * pairs * owned * peers
    norm_ref[...] = jnp.sqrt(total[:, :1] / entries)


def shards(
    state, hamiltonian, mode_rates, ado_modes, link_src, link_site, link_coef, send_ids, step_units
):
    groups = lax.axis_size("grp")
    members = lax.axis_size("dev")
    sites, owned = state.shape[1], state.shape[3]
    links = link_src.shape[0]
    received = send_ids.shape[1]
    asks = received * USES
    wide = links * owned
    pairs = sites * sites
    width = -(-4 * sites // 128) * 128
    turns = len(ERRORS)
    vmem = pl.BlockSpec(memory_space=pltpu.VMEM)
    hbm = pl.BlockSpec(memory_space=pltpu.HBM)
    increment, norm = pl.pallas_call(
        functools.partial(kernel, groups, members),
        out_shape=(
            jax.ShapeDtypeStruct(state.shape, F32),
            jax.ShapeDtypeStruct((1, 1), F32),
        ),
        in_specs=[hbm] * 9,
        out_specs=(vmem, vmem),
        scratch_shapes=[
            pltpu.VMEM(hamiltonian.shape, F32),
            pltpu.VMEM((1, mode_rates.shape[0]), F32),
            pltpu.VMEM(ado_modes.shape, jnp.int32),
            pltpu.VMEM(link_src.shape, jnp.int32),
            pltpu.VMEM(link_site.shape, jnp.int32),
            pltpu.VMEM(link_coef.shape, F32),
            pltpu.VMEM(send_ids.shape, jnp.int32),
            pltpu.SMEM((1, 1), jnp.int32),
            pltpu.VMEM((len(ERRORS) + 1,) + state.shape, F32),
            pltpu.VMEM(state.shape, F32),
            pltpu.VMEM((2 * pairs, pairs), BF16),
            pltpu.VMEM((2 * owned, asks), BF16),
            pltpu.VMEM((2 * owned, wide), BF16),
            pltpu.VMEM((asks, wide), F32),
            pltpu.VMEM((2 * asks, owned), BF16),
            pltpu.VMEM((2, sites, sites, wide), F32),
            pltpu.VMEM((sites, 1, asks), F32),
            pltpu.VMEM((sites, asks), F32),
            pltpu.VMEM((sites, 1, asks), F32),
            pltpu.VMEM((sites, asks), F32),
            pltpu.VMEM((2, sites, sites, asks), F32),
            pltpu.VMEM((2, sites, asks), F32),
            pltpu.VMEM((2 * pairs, 2 * owned), BF16),
            pltpu.VMEM((2, sites, sites, wide), F32),
            pltpu.VMEM((2, sites, asks), F32),
            pltpu.VMEM((asks, width), F32),
            pltpu.VMEM((turns, asks, width), F32),
            pltpu.VMEM((2, groups * members, 1, 128), F32),
            pltpu.VMEM((2, groups * members, 1, 128), F32),
            pltpu.SemaphoreType.DMA((9,)),
            pltpu.SemaphoreType.DMA((turns,)),
            pltpu.SemaphoreType.DMA((turns,)),
            pltpu.SemaphoreType.DMA((2,)),
            pltpu.SemaphoreType.DMA((2,)),
        ],
        compiler_params=pltpu.CompilerParams(
            collective_id=0, has_side_effects=True, vmem_limit_bytes=64 * 1024 * 1024
        ),
    )(
        state,
        hamiltonian,
        mode_rates.reshape(1, -1),
        ado_modes,
        link_src,
        link_site,
        link_coef,
        send_ids,
        step_units.reshape(1, 1),
    )
    return state + increment, norm.reshape(())


def solution(mesh):
    return jax.shard_map(
        shards,
        mesh=mesh,
        in_specs=(
            P(None, None, None, ("grp", "dev")),
            P(),
            P(),
            P(None, ("grp", "dev")),
            P(None, ("grp", "dev")),
            P(None, ("grp", "dev")),
            P(None, None, ("grp", "dev")),
            P(("grp", "dev"), None),
            P(),
        ),
        out_specs=(P(None, None, None, ("grp", "dev")), P()),
        check_vma=False,
    )
```

```python
import functools
from fractions import Fraction as Q

import jax
import jax.numpy as jnp
from jax import lax
from jax.experimental import pallas as pl
from jax.experimental.pallas import tpu as pltpu
from jax.sharding import PartitionSpec as P

TABLEAU = (
    (Q(1, 5),),
    (Q(3, 40), Q(9, 40)),
    (Q(44, 45), Q(-56, 15), Q(32, 9)),
    (Q(19372, 6561), Q(-25360, 2187), Q(64448, 6561), Q(-212, 729)),
    (Q(9017, 3168), Q(-355, 33), Q(46732, 5247), Q(49, 176), Q(-5103, 18656)),
    (Q(35, 384), Q(0), Q(500, 1113), Q(125, 192), Q(-2187, 6784), Q(11, 84)),
)
ERRORS = (Q(71, 57600), Q(0), Q(-71, 16695), Q(71, 1920), Q(-17253, 339200), Q(22, 525), Q(-1, 40))
ABS_TOL = 0.001
REL_TOL = 0.01
UNIT_STEP = 1.0 / 64
USES = 4
HIGHEST = lax.Precision.HIGHEST
MESH = pl.DeviceIdType.MESH
F32 = jnp.float32
BF16 = jnp.bfloat16


def step_polynomials():
    degree = len(ERRORS) + 1

    def combine(weights, sections, constant):
        total = [Q(constant)] + [Q(0)] * (degree - 1)
        for weight, section in zip(weights, sections):
            total = [t + weight * s for t, s in zip(total, section)]
        return total

    def advance(poly):
        return [Q(0)] + poly[:-1]

    sections = [advance(combine((), (), 1))]
    inner = None
    for weights in TABLEAU:
        inner = combine(weights, sections, 1)
        sections.append(advance(inner))
    error = combine(ERRORS, sections, 0)
    return [float(c) for c in inner], [float(c) for c in error]


NEW_POLY, ERR_POLY = step_polynomials()


def one_hot(condition, dtype):
    return jnp.where(condition, 1.0, 0.0).astype(dtype)


def iota(shape, dim):
    return lax.broadcasted_iota(jnp.int32, shape, dim)


def split(values):
    high = values.astype(BF16)
    return high, (values - high.astype(F32)).astype(BF16)


def dot(lhs, rhs):
    return jnp.dot(lhs, rhs, preferred_element_type=F32)


def dot_nt(lhs, rhs, precision=None):
    return lax.dot_general(
        lhs, rhs, (((1,), (1,)), ((), ())), precision=precision, preferred_element_type=F32
    )


def kernel(
    groups,
    members,
    state_hbm,
    ham_hbm,
    rates_hbm,
    modes_hbm,
    src_hbm,
    site_hbm,
    coef_hbm,
    ids_hbm,
    units_hbm,
    out_ref,
    norm_ref,
    ham_ref,
    rates_ref,
    modes_ref,
    src_ref,
    site_ref,
    coef_ref,
    ids_ref,
    units_ref,
    power_ref,
    part_ref,
    super_ref,
    pick_ref,
    select_ref,
    request_ref,
    spread_ref,
    weight_ref,
    own_row_ref,
    own_col_ref,
    asked_row_ref,
    asked_col_ref,
    chosen_ref,
    cols_ref,
    halves_ref,
    arrived_ref,
    fetched_ref,
    tr_ref,
    send_ref,
    recv_ref,
    note_ref,
    noted_ref,
    load_sem,
    send_sem,
    recv_sem,
    note_send_sem,
    note_recv_sem,
):
    peers = groups * members
    sites = state_hbm.shape[1]
    owned = state_hbm.shape[3]
    links = src_ref.shape[0]
    received = ids_ref.shape[1]
    wide = links * owned
    asks = received * USES
    rows = asks // peers
    pairs = sites * sites
    width = send_ref.shape[1]
    my_grp, my_dev = lax.axis_index("grp"), lax.axis_index("dev")
    me = my_grp * members + my_dev

    def wrap(value, size):
        return jnp.where(value >= size, value - size, value)

    def each_peer(visit, unroll=False):
        for jump in range(1, groups):
            visit(wrap(my_grp + jump, groups), my_dev)

        def ring(step, carry):
            dev = wrap(my_dev + step, members)
            for jump in range(groups):
                visit(wrap(my_grp + jump, groups), dev)
            return carry

        if unroll:
            for step in range(1, members):
                ring(step, 0)
        else:
            lax.fori_loop(1, members, ring, 0)

    barrier = pltpu.get_barrier_semaphore()

    def greet(grp, dev):
        pl.semaphore_signal(barrier, inc=1, device_id=(grp, dev), device_id_type=MESH)

    loads = [
        pltpu.make_async_copy(source, target, load_sem.at[place])
        for place, (source, target) in enumerate(
            (
                (src_hbm, src_ref),
                (site_hbm, site_ref),
                (coef_hbm, coef_ref),
                (units_hbm, units_ref),
                (ham_hbm, ham_ref),
                (rates_hbm, rates_ref),
                (modes_hbm, modes_ref),
                (ids_hbm, ids_ref),
                (state_hbm, part_ref),
            )
        )
    ]
    for load in loads:
        load.start()
    each_peer(greet)

    def send_all(turn):
        mine = pl.ds(pl.multiple_of(me * rows, rows), rows)

        def send(grp, dev):
            peer = grp * members + dev
            pltpu.make_async_remote_copy(
                src_ref=send_ref.at[pl.ds(pl.multiple_of(peer * rows, rows), rows)],
                dst_ref=recv_ref.at[turn - 1, mine],
                send_sem=send_sem.at[turn - 1],
                recv_sem=recv_sem.at[turn - 1],
                device_id=(grp, dev),
                device_id_type=MESH,
            ).start()

        each_peer(send, unroll=True)
        recv_ref[turn - 1, mine] = send_ref[mine]

    def bulk(turn, sem):
        every = pl.ds(0, (peers - 1) * rows)
        return pltpu.make_async_copy(send_ref.at[every], recv_ref.at[turn, every], sem.at[turn])

    def wait_all(turn):
        bulk(turn - 1, recv_sem).wait()
        bulk(turn - 1, send_sem).wait()

    def send_note(note):
        def send(grp, dev):
            pltpu.make_async_remote_copy(
                src_ref=note_ref.at[note, grp * members + dev],
                dst_ref=noted_ref.at[note, me],
                send_sem=note_send_sem.at[note],
                recv_sem=note_recv_sem.at[note],
                device_id=(grp, dev),
                device_id_type=MESH,
            ).start()

        each_peer(send)
        noted_ref[note, me] = note_ref[note, me]

    def wait_note(note):
        every = pl.ds(0, peers - 1)
        for sem in (note_recv_sem, note_send_sem):
            pltpu.make_async_copy(
                note_ref.at[note, every], noted_ref.at[note, every], sem.at[note]
            ).wait()

    earlier = one_hot(iota((owned, owned), 0) < iota((owned, owned), 1), BF16)
    base = jnp.zeros((received, 1), F32)
    wanted = jnp.zeros((asks, owned), F32)
    place = jnp.zeros((asks, owned), F32)
    loads[0].wait()
    loads[1].wait()
    for link in range(links):
        lanes = slice(link * owned, (link + 1) * owned)
        source = src_ref[link : link + 1, :]
        site = site_ref[link : link + 1, :]
        hit = iota((received, owned), 0) == source - owned
        hits = one_hot(hit, F32)
        before = dot(one_hot(hit, BF16), earlier) + base
        rank = jnp.sum(hits * before, axis=0, keepdims=True).astype(jnp.int32)
        base = base + jnp.sum(hits, axis=1, keepdims=True)
        ask = jnp.where(source >= owned, (source - owned) * USES + rank, -1)
        asking = iota((asks, owned), 0) == ask
        wanted = wanted + jnp.where(asking, site.astype(F32), 0.0)
        request = one_hot(asking, F32)
        request_ref[:, lanes] = request
        place = place + request
        local = one_hot(iota((owned, owned), 0) == source, BF16)
        select_ref[:owned, lanes] = local
        select_ref[owned:, lanes] = local
    lane_of = iota((peers, rows, 128), 1) == iota((peers, rows, 128), 2)
    lane_of = one_hot(lane_of, F32).reshape(asks, 128)
    peer_of = iota((peers, rows, peers), 0) == iota((peers, rows, peers), 2)
    peer_of = one_hot(peer_of, F32).reshape(asks, peers)
    wanted = jnp.sum(wanted, axis=1, keepdims=True) * lane_of
    wanted = wanted.reshape(peers, rows, 128).sum(axis=1, keepdims=True)
    note_ref[0] = wanted
    pl.semaphore_wait(barrier, peers - 1)
    send_note(0)

    place = place.astype(BF16)
    for start in (0, asks):
        spread_ref[start : start + asks, asks:] = place
    for load in loads[2:]:
        load.wait()
    step_size = units_ref[0, 0].astype(F32) * UNIT_STEP

    def flat(ref):
        return jnp.concatenate([ref[link : link + 1, :] for link in range(links)], axis=1)

    table = [flat(coef_ref.at[k]) * step_size for k in range(4)]
    table = table + [flat(site_ref).astype(F32), jnp.zeros((3, wide), F32)]
    table = dot_nt(jnp.concatenate(table, axis=0), request_ref[...], HIGHEST)
    left_real, left_imag = table[0:1], table[1:2]
    right_real, right_imag = table[2:3], table[3:4]
    own_site = jnp.round(table[4:5]).astype(jnp.int32)
    own_col_ref[...] = one_hot(iota((sites, asks), 0) == own_site, F32)
    own_row_ref[...] = one_hot(iota((sites, 1, asks), 0) == own_site[None], F32)
    for link in range(links):
        lanes = slice(link * owned, (link + 1) * owned)
        site = site_ref[link : link + 1, :]
        for part in range(2):
            left = coef_ref[part, link : link + 1, :] * step_size
            right = coef_ref[part + 2, link : link + 1, :] * step_size
            right = jnp.where(iota((sites, owned), 0) == site, right, 0.0)
            for row in range(sites):
                weight_ref[part, row, :, lanes] = jnp.where(site == row, left, 0.0) - right
    first = one_hot(iota((sites, sites, sites), 0) == iota((sites, sites, sites), 2), F32)
    second = one_hot(iota((sites, sites, sites), 1) == iota((sites, sites, sites), 2), F32)
    first, second = (hot.reshape(pairs, sites).astype(BF16) for hot in (first, second))
    ham = ham_ref[...] * (0.5 * step_size)

    def pieces(values):
        high, low = split(values)
        middle = high.astype(F32) + low.astype(F32)
        return high, low, (values - middle).astype(BF16)

    def lifted(hot):
        half = functools.reduce(
            jnp.add, [dot(hot, piece) + dot_nt(hot, piece) for piece in pieces(ham)]
        )
        return functools.reduce(jnp.add, [dot_nt(piece, hot) for piece in pieces(half)])

    same_first, same_second = dot_nt(first, first), dot_nt(second, second)
    operator = lifted(first) * same_second - lifted(second) * same_first
    high, low = split(operator)
    super_ref[:pairs] = high
    super_ref[pairs:] = low
    modes = rates_ref.shape[1]
    counts = jnp.zeros((modes, owned), F32)
    for depth in range(modes_ref.shape[0]):
        counts = counts + one_hot(iota((modes, owned), 0) == modes_ref[depth : depth + 1, :], F32)
    rates = jnp.broadcast_to(rates_ref[...], (8, modes))
    decay = jnp.dot(rates, counts, precision=HIGHEST, preferred_element_type=F32)[0:1] * step_size
    spread_low = iota((received, asks), 0) * USES
    spread_at = iota((received, asks), 1)
    spread = one_hot((spread_at >= spread_low) & (spread_at < spread_low + USES), BF16)
    ids = jnp.broadcast_to(ids_ref[...].astype(F32), (16, received)).astype(BF16)
    ids = dot(ids, spread)[0:1].astype(jnp.int32)
    picks = one_hot(iota((owned, asks), 0) == ids, BF16)
    pick_ref[:owned] = picks
    pick_ref[owned:] = picks
    relay = dot(place, picks).astype(BF16)
    for start in (0, asks):
        spread_ref[start : start + asks, :asks] = relay

    def prepare():
        high, low = split(part_ref[...].reshape(2 * pairs, owned))
        chosen_ref[...] = dot(jnp.concatenate([high, low], axis=1), pick_ref[...]).reshape(
            2, sites, sites, asks
        )

    prepare()
    arrived_ref[...] = jnp.zeros(arrived_ref.shape, BF16)

    wait_note(0)
    asked = dot(peer_of.astype(BF16), noted_ref[0].reshape(peers, 128).astype(BF16))
    asked = jnp.broadcast_to(jnp.sum(asked * lane_of, axis=1, keepdims=True), (asks, 128))
    asked = asked.T[0:1].astype(jnp.int32)
    asked_col_ref[...] = one_hot(iota((sites, asks), 0) == asked, F32)
    asked_row_ref[...] = one_hot(iota((sites, 1, asks), 0) == asked[None], F32)

    def advance(turn, carry):
        before = turn - 1
        relayed = dot(arrived_ref[...], spread_ref[:, :asks]).reshape(2, sites, sites, asks)
        col_mask = asked_col_ref[...]
        picked = []
        for part in range(2):
            total = jnp.zeros((sites, asks), F32)
            for row in range(sites):
                block = chosen_ref[part, row] + relayed[part, row]
                total = total + block * asked_row_ref[row]
                cols_ref[part, row : row + 1, :] = jnp.sum(block * col_mask, axis=0, keepdims=True)
            picked.append(total)
        outgoing = jnp.concatenate(
            picked
            + [cols_ref[...].reshape(2 * sites, asks), jnp.zeros((width - 4 * sites, asks), F32)],
            axis=0,
        )
        send_ref[...] = outgoing.T
        send_all(turn)

        far = dot(arrived_ref[...], spread_ref[:, asks:]).reshape(2, sites, sites, owned)
        current = part_ref[...] + far
        power_ref[before] = current
        high, low = split(current.reshape(2 * pairs, owned))
        halves_ref[...] = jnp.concatenate([high, low], axis=1)
        fetched_ref[...] = dot(halves_ref[...], select_ref[...]).reshape(2, sites, sites, wide)
        high = jnp.concatenate([halves_ref[:pairs, :owned], halves_ref[pairs:, :owned]], axis=1)
        low = jnp.concatenate([halves_ref[:pairs, owned:], halves_ref[pairs:, owned:]], axis=1)
        both = dot(super_ref[...], high)
        bracket = both[:pairs] + both[pairs:] + dot(super_ref[:pairs], low)
        part_ref[0] = (
            bracket[:, owned:].reshape(sites, sites, owned) - decay * power_ref[before, 0]
        )
        part_ref[1] = (
            -bracket[:, :owned].reshape(sites, sites, owned) - decay * power_ref[before, 1]
        )

        def near(row, carry):
            real, imag = part_ref[0, row], part_ref[1, row]
            for link in range(links):
                lanes = slice(link * owned, (link + 1) * owned)
                weight_real, weight_imag = (weight_ref[k, row, :, lanes] for k in range(2))
                source_real, source_imag = (fetched_ref[k, row, :, lanes] for k in range(2))
                real = real + (weight_real * source_imag + weight_imag * source_real)
                imag = imag + (weight_imag * source_imag - weight_real * source_real)
            part_ref[0, row] = real
            part_ref[1, row] = imag
            return carry

        lax.fori_loop(0, sites, near, 0)
        prepare()

        wait_all(turn)
        found = recv_ref[turn - 1].T
        row_real, row_imag = found[:sites], found[sites : 2 * sites]
        col_real, col_imag = found[2 * sites : 3 * sites], found[3 * sites : 4 * sites]
        tl = (
            left_real * row_imag + left_imag * row_real,
            left_imag * row_imag - left_real * row_real,
        )
        tr_ref[0] = -(right_real * col_imag + right_imag * col_real)
        tr_ref[1] = right_real * col_real - right_imag * col_imag
        own_col = own_col_ref[...]
        blocks = [
            tl[part] * own_row_ref[row] + own_col * tr_ref[part, row : row + 1, :]
            for part in range(2)
            for row in range(sites)
        ]
        high, low = split(jnp.concatenate(blocks, axis=0))
        arrived_ref[...] = jnp.concatenate([high, low], axis=1)
        return carry

    turns = len(ERRORS)
    lax.fori_loop(1, turns + 1, advance, 0)
    far = dot(arrived_ref[...], spread_ref[:, asks:]).reshape(2, sites, sites, owned)
    power_ref[turns] = part_ref[...] + far

    def combine(poly):
        terms = [
            power_ref[k] if c == 1.0 else power_ref[k] * c for k, c in enumerate(poly) if c != 0.0
        ]
        return functools.reduce(jnp.add, terms)

    increment = combine([0.0] + NEW_POLY[1:])
    out_ref[...] = increment
    new_state = power_ref[0] + increment
    scale = ABS_TOL + REL_TOL * jnp.maximum(jnp.abs(power_ref[0]), jnp.abs(new_state))
    ratio = combine(ERR_POLY) / scale
    tile = jnp.sum((ratio * ratio).reshape(2 * pairs // 8, 8, owned), axis=0)
    tile = jnp.sum(tile, axis=0, keepdims=True)
    tile = jnp.sum(tile, axis=1, keepdims=True)
    note_ref[1] = jnp.broadcast_to(tile[None], (peers, 1, 128))
    send_note(1)
    wait_note(1)
    total = jnp.sum(noted_ref[1], axis=0)
    entries = 2 * pairs * owned * peers
    norm_ref[...] = jnp.sqrt(total[:, :1] / entries)


def shards(
    state, hamiltonian, mode_rates, ado_modes, link_src, link_site, link_coef, send_ids, step_units
):
    groups = lax.axis_size("grp")
    members = lax.axis_size("dev")
    sites, owned = state.shape[1], state.shape[3]
    links = link_src.shape[0]
    received = send_ids.shape[1]
    asks = received * USES
    wide = links * owned
    pairs = sites * sites
    width = -(-4 * sites // 128) * 128
    turns = len(ERRORS)
    vmem = pl.BlockSpec(memory_space=pltpu.VMEM)
    hbm = pl.BlockSpec(memory_space=pltpu.HBM)
    increment, norm = pl.pallas_call(
        functools.partial(kernel, groups, members),
        out_shape=(
            jax.ShapeDtypeStruct(state.shape, F32),
            jax.ShapeDtypeStruct((1, 1), F32),
        ),
        in_specs=[hbm] * 9,
        out_specs=(vmem, vmem),
        scratch_shapes=[
            pltpu.VMEM(hamiltonian.shape, F32),
            pltpu.VMEM((1, mode_rates.shape[0]), F32),
            pltpu.VMEM(ado_modes.shape, jnp.int32),
            pltpu.VMEM(link_src.shape, jnp.int32),
            pltpu.VMEM(link_site.shape, jnp.int32),
            pltpu.VMEM(link_coef.shape, F32),
            pltpu.VMEM(send_ids.shape, jnp.int32),
            pltpu.SMEM((1, 1), jnp.int32),
            pltpu.VMEM((len(ERRORS) + 1,) + state.shape, F32),
            pltpu.VMEM(state.shape, F32),
            pltpu.VMEM((2 * pairs, pairs), BF16),
            pltpu.VMEM((2 * owned, asks), BF16),
            pltpu.VMEM((2 * owned, wide), BF16),
            pltpu.VMEM((asks, wide), F32),
            pltpu.VMEM((2 * asks, asks + owned), BF16),
            pltpu.VMEM((2, sites, sites, wide), F32),
            pltpu.VMEM((sites, 1, asks), F32),
            pltpu.VMEM((sites, asks), F32),
            pltpu.VMEM((sites, 1, asks), F32),
            pltpu.VMEM((sites, asks), F32),
            pltpu.VMEM((2, sites, sites, asks), F32),
            pltpu.VMEM((2, sites, asks), F32),
            pltpu.VMEM((2 * pairs, 2 * owned), BF16),
            pltpu.VMEM((2 * pairs, 2 * asks), BF16),
            pltpu.VMEM((2, sites, sites, wide), F32),
            pltpu.VMEM((2, sites, asks), F32),
            pltpu.VMEM((asks, width), F32),
            pltpu.VMEM((turns, asks, width), F32),
            pltpu.VMEM((2, groups * members, 1, 128), F32),
            pltpu.VMEM((2, groups * members, 1, 128), F32),
            pltpu.SemaphoreType.DMA((9,)),
            pltpu.SemaphoreType.DMA((turns,)),
            pltpu.SemaphoreType.DMA((turns,)),
            pltpu.SemaphoreType.DMA((2,)),
            pltpu.SemaphoreType.DMA((2,)),
        ],
        compiler_params=pltpu.CompilerParams(
            collective_id=0, has_side_effects=True, vmem_limit_bytes=64 * 1024 * 1024
        ),
    )(
        state,
        hamiltonian,
        mode_rates.reshape(1, -1),
        ado_modes,
        link_src,
        link_site,
        link_coef,
        send_ids,
        step_units.reshape(1, 1),
    )
    return state + increment, norm.reshape(())


def solution(mesh):
    return jax.shard_map(
        shards,
        mesh=mesh,
        in_specs=(
            P(None, None, None, ("grp", "dev")),
            P(),
            P(),
            P(None, ("grp", "dev")),
            P(None, ("grp", "dev")),
            P(None, ("grp", "dev")),
            P(None, None, ("grp", "dev")),
            P(("grp", "dev"), None),
            P(),
        ),
        out_specs=(P(None, None, None, ("grp", "dev")), P()),
        check_vma=False,
    )
```

```python
import functools
from fractions import Fraction as Q

import jax
import jax.numpy as jnp
from jax import lax
from jax.experimental import pallas as pl
from jax.experimental.pallas import tpu as pltpu
from jax.sharding import PartitionSpec as P

TABLEAU = (
    (Q(1, 5),),
    (Q(3, 40), Q(9, 40)),
    (Q(44, 45), Q(-56, 15), Q(32, 9)),
    (Q(19372, 6561), Q(-25360, 2187), Q(64448, 6561), Q(-212, 729)),
    (Q(9017, 3168), Q(-355, 33), Q(46732, 5247), Q(49, 176), Q(-5103, 18656)),
    (Q(35, 384), Q(0), Q(500, 1113), Q(125, 192), Q(-2187, 6784), Q(11, 84)),
)
ERRORS = (Q(71, 57600), Q(0), Q(-71, 16695), Q(71, 1920), Q(-17253, 339200), Q(22, 525), Q(-1, 40))
ABS_TOL = 0.001
REL_TOL = 0.01
UNIT_STEP = 1.0 / 64
USES = 4
HIGHEST = lax.Precision.HIGHEST
MESH = pl.DeviceIdType.MESH
F32 = jnp.float32
BF16 = jnp.bfloat16


def folding(rows, values, width):
    spare = width - values
    pieces = values // spare if spare else 0
    if not pieces or values % spare:
        return rows, 0, ()
    dropped = rows // (pieces + 1)
    kept = rows - dropped
    return kept, spare, [(k, kept + k // pieces, k % pieces) for k in range(dropped * pieces)]


def step_polynomials():
    degree = len(ERRORS) + 1

    def combine(weights, sections, constant):
        total = [Q(constant)] + [Q(0)] * (degree - 1)
        for weight, section in zip(weights, sections):
            total = [t + weight * s for t, s in zip(total, section)]
        return total

    def advance(poly):
        return [Q(0)] + poly[:-1]

    sections = [advance(combine((), (), 1))]
    inner = None
    for weights in TABLEAU:
        inner = combine(weights, sections, 1)
        sections.append(advance(inner))
    error = combine(ERRORS, sections, 0)
    return [float(c) for c in inner], [float(c) for c in error]


NEW_POLY, ERR_POLY = step_polynomials()


def one_hot(condition, dtype):
    return jnp.where(condition, 1.0, 0.0).astype(dtype)


def iota(shape, dim):
    return lax.broadcasted_iota(jnp.int32, shape, dim)


def split(values):
    high = values.astype(BF16)
    return high, (values - high.astype(F32)).astype(BF16)


def dot(lhs, rhs):
    return jnp.dot(lhs, rhs, preferred_element_type=F32)


def dot_nt(lhs, rhs, precision=None):
    return lax.dot_general(
        lhs, rhs, (((1,), (1,)), ((), ())), precision=precision, preferred_element_type=F32
    )


def kernel(
    groups,
    members,
    state_hbm,
    ham_hbm,
    rates_hbm,
    modes_hbm,
    src_hbm,
    site_hbm,
    coef_hbm,
    ids_hbm,
    units_hbm,
    out_ref,
    norm_ref,
    ham_ref,
    rates_ref,
    modes_ref,
    src_ref,
    site_ref,
    coef_ref,
    ids_ref,
    units_ref,
    power_ref,
    part_ref,
    super_ref,
    pick_ref,
    select_ref,
    request_ref,
    spread_ref,
    weight_ref,
    own_row_ref,
    own_col_ref,
    asked_row_ref,
    asked_col_ref,
    chosen_ref,
    cols_ref,
    halves_ref,
    arrived_ref,
    fetched_ref,
    tr_ref,
    send_ref,
    full_ref,
    recv_ref,
    note_ref,
    noted_ref,
    load_sem,
    send_sem,
    recv_sem,
    note_send_sem,
    note_recv_sem,
):
    peers = groups * members
    sites = state_hbm.shape[1]
    owned = state_hbm.shape[3]
    links = src_ref.shape[0]
    received = ids_ref.shape[1]
    wide = links * owned
    asks = received * USES
    rows = asks // peers
    pairs = sites * sites
    width = send_ref.shape[2]
    kept, spare, moves = folding(rows, 4 * sites, width)
    turn_of_lane = lax.rem(iota((max(spare, 1), asks), 1), rows)
    my_grp, my_dev = lax.axis_index("grp"), lax.axis_index("dev")
    me = my_grp * members + my_dev

    def wrap(value, size):
        return jnp.where(value >= size, value - size, value)

    def each_peer(visit, unroll=False):
        for jump in range(1, groups):
            visit(wrap(my_grp + jump, groups), my_dev)

        def ring(step, carry):
            dev = wrap(my_dev + step, members)
            for jump in range(groups):
                visit(wrap(my_grp + jump, groups), dev)
            return carry

        if unroll:
            for step in range(1, members):
                ring(step, 0)
        else:
            lax.fori_loop(1, members, ring, 0)

    barrier = pltpu.get_barrier_semaphore()

    def greet(grp, dev):
        pl.semaphore_signal(barrier, inc=1, device_id=(grp, dev), device_id_type=MESH)

    loads = [
        pltpu.make_async_copy(source, target, load_sem.at[place])
        for place, (source, target) in enumerate(
            (
                (src_hbm, src_ref),
                (site_hbm, site_ref),
                (coef_hbm, coef_ref),
                (units_hbm, units_ref),
                (ham_hbm, ham_ref),
                (rates_hbm, rates_ref),
                (modes_hbm, modes_ref),
                (ids_hbm, ids_ref),
                (state_hbm, part_ref),
            )
        )
    ]
    for load in loads:
        load.start()
    each_peer(greet)

    def send_all(turn):
        def send(grp, dev):
            pltpu.make_async_remote_copy(
                src_ref=send_ref.at[grp * members + dev],
                dst_ref=recv_ref.at[turn - 1, me],
                send_sem=send_sem.at[turn - 1],
                recv_sem=recv_sem.at[turn - 1],
                device_id=(grp, dev),
                device_id_type=MESH,
            ).start()

        each_peer(send, unroll=True)
        recv_ref[turn - 1, me] = send_ref[me]

    def bulk(turn, sem):
        every = pl.ds(0, peers - 1)
        return pltpu.make_async_copy(send_ref.at[every], recv_ref.at[turn, every], sem.at[turn])

    def wait_all(turn):
        bulk(turn - 1, recv_sem).wait()
        bulk(turn - 1, send_sem).wait()

    def send_note(note):
        def send(grp, dev):
            pltpu.make_async_remote_copy(
                src_ref=note_ref.at[note, grp * members + dev],
                dst_ref=noted_ref.at[note, me],
                send_sem=note_send_sem.at[note],
                recv_sem=note_recv_sem.at[note],
                device_id=(grp, dev),
                device_id_type=MESH,
            ).start()

        each_peer(send)
        noted_ref[note, me] = note_ref[note, me]

    def wait_note(note):
        every = pl.ds(0, peers - 1)
        for sem in (note_recv_sem, note_send_sem):
            pltpu.make_async_copy(
                note_ref.at[note, every], noted_ref.at[note, every], sem.at[note]
            ).wait()

    earlier = one_hot(iota((owned, owned), 0) < iota((owned, owned), 1), BF16)
    base = jnp.zeros((received, 1), F32)
    wanted = jnp.zeros((asks, owned), F32)
    place = jnp.zeros((asks, owned), F32)
    loads[0].wait()
    loads[1].wait()
    for link in range(links):
        lanes = slice(link * owned, (link + 1) * owned)
        source = src_ref[link : link + 1, :]
        site = site_ref[link : link + 1, :]
        hit = iota((received, owned), 0) == source - owned
        hits = one_hot(hit, F32)
        before = dot(one_hot(hit, BF16), earlier) + base
        rank = jnp.sum(hits * before, axis=0, keepdims=True).astype(jnp.int32)
        base = base + jnp.sum(hits, axis=1, keepdims=True)
        ask = jnp.where(source >= owned, (source - owned) * USES + rank, -1)
        asking = iota((asks, owned), 0) == ask
        wanted = wanted + jnp.where(asking, site.astype(F32), 0.0)
        request = one_hot(asking, F32)
        request_ref[:, lanes] = request
        place = place + request
        local = one_hot(iota((owned, owned), 0) == source, BF16)
        select_ref[:owned, lanes] = local
        select_ref[owned:, lanes] = local
    lane_of = iota((peers, rows, 128), 1) == iota((peers, rows, 128), 2)
    lane_of = one_hot(lane_of, F32).reshape(asks, 128)
    peer_of = iota((peers, rows, peers), 0) == iota((peers, rows, peers), 2)
    peer_of = one_hot(peer_of, F32).reshape(asks, peers)
    wanted = jnp.sum(wanted, axis=1, keepdims=True) * lane_of
    wanted = wanted.reshape(peers, rows, 128).sum(axis=1, keepdims=True)
    note_ref[0] = wanted
    pl.semaphore_wait(barrier, peers - 1)
    send_note(0)

    place = place.astype(BF16)
    for start in (0, asks):
        spread_ref[start : start + asks, asks:] = place
    for load in loads[2:]:
        load.wait()
    step_size = units_ref[0, 0].astype(F32) * UNIT_STEP

    def flat(ref):
        return jnp.concatenate([ref[link : link + 1, :] for link in range(links)], axis=1)

    table = [flat(coef_ref.at[k]) * step_size for k in range(4)]
    table = table + [flat(site_ref).astype(F32), jnp.zeros((3, wide), F32)]
    table = dot_nt(jnp.concatenate(table, axis=0), request_ref[...], HIGHEST)
    left_real, left_imag = table[0:1], table[1:2]
    right_real, right_imag = table[2:3], table[3:4]
    own_site = jnp.round(table[4:5]).astype(jnp.int32)
    own_col_ref[...] = one_hot(iota((sites, asks), 0) == own_site, F32)
    own_row_ref[...] = one_hot(iota((sites, 1, asks), 0) == own_site[None], F32)
    for link in range(links):
        lanes = slice(link * owned, (link + 1) * owned)
        site = site_ref[link : link + 1, :]
        for part in range(2):
            left = coef_ref[part, link : link + 1, :] * step_size
            right = coef_ref[part + 2, link : link + 1, :] * step_size
            right = jnp.where(iota((sites, owned), 0) == site, right, 0.0)
            for row in range(sites):
                weight_ref[part, row, :, lanes] = jnp.where(site == row, left, 0.0) - right
    first = one_hot(iota((sites, sites, sites), 0) == iota((sites, sites, sites), 2), F32)
    second = one_hot(iota((sites, sites, sites), 1) == iota((sites, sites, sites), 2), F32)
    first, second = (hot.reshape(pairs, sites).astype(BF16) for hot in (first, second))
    ham = ham_ref[...] * (0.5 * step_size)

    def pieces(values):
        high, low = split(values)
        middle = high.astype(F32) + low.astype(F32)
        return high, low, (values - middle).astype(BF16)

    def lifted(hot):
        half = functools.reduce(
            jnp.add, [dot(hot, piece) + dot_nt(hot, piece) for piece in pieces(ham)]
        )
        return functools.reduce(jnp.add, [dot_nt(piece, hot) for piece in pieces(half)])

    same_first, same_second = dot_nt(first, first), dot_nt(second, second)
    operator = lifted(first) * same_second - lifted(second) * same_first
    high, low = split(operator)
    super_ref[:pairs] = high
    super_ref[pairs:] = low
    modes = rates_ref.shape[1]
    counts = jnp.zeros((modes, owned), F32)
    for depth in range(modes_ref.shape[0]):
        counts = counts + one_hot(iota((modes, owned), 0) == modes_ref[depth : depth + 1, :], F32)
    rates = jnp.broadcast_to(rates_ref[...], (8, modes))
    decay = jnp.dot(rates, counts, precision=HIGHEST, preferred_element_type=F32)[0:1] * step_size
    spread_low = iota((received, asks), 0) * USES
    spread_at = iota((received, asks), 1)
    spread = one_hot((spread_at >= spread_low) & (spread_at < spread_low + USES), BF16)
    ids = jnp.broadcast_to(ids_ref[...].astype(F32), (16, received)).astype(BF16)
    ids = dot(ids, spread)[0:1].astype(jnp.int32)
    picks = one_hot(iota((owned, asks), 0) == ids, BF16)
    pick_ref[:owned] = picks
    pick_ref[owned:] = picks
    relay = dot(place, picks).astype(BF16)
    for start in (0, asks):
        spread_ref[start : start + asks, :asks] = relay

    def prepare():
        high, low = split(part_ref[...].reshape(2 * pairs, owned))
        chosen_ref[...] = dot(jnp.concatenate([high, low], axis=1), pick_ref[...]).reshape(
            2, sites, sites, asks
        )

    prepare()
    arrived_ref[...] = jnp.zeros(arrived_ref.shape, BF16)
    full_ref[...] = jnp.zeros(full_ref.shape, F32)

    wait_note(0)
    asked = dot(peer_of.astype(BF16), noted_ref[0].reshape(peers, 128).astype(BF16))
    asked = jnp.broadcast_to(jnp.sum(asked * lane_of, axis=1, keepdims=True), (asks, 128))
    asked = asked.T[0:1].astype(jnp.int32)
    asked_col_ref[...] = one_hot(iota((sites, asks), 0) == asked, F32)
    asked_row_ref[...] = one_hot(iota((sites, 1, asks), 0) == asked[None], F32)

    def advance(turn, carry):
        before = turn - 1
        relayed = dot(arrived_ref[...], spread_ref[:, :asks]).reshape(2, sites, sites, asks)
        col_mask = asked_col_ref[...]
        picked = []
        for part in range(2):
            total = jnp.zeros((sites, asks), F32)
            for row in range(sites):
                block = chosen_ref[part, row] + relayed[part, row]
                total = total + block * asked_row_ref[row]
                cols_ref[part, row : row + 1, :] = jnp.sum(block * col_mask, axis=0, keepdims=True)
            picked.append(total)
        outgoing = jnp.concatenate(picked + [cols_ref[...].reshape(2 * sites, asks)], axis=0)
        if spare:
            extra = jnp.zeros((spare, asks), F32)
            for keep, drop, piece in moves:
                moved = outgoing[piece * spare : (piece + 1) * spare]
                moved = pltpu.roll(moved, asks - (drop - keep), 1)
                extra = jnp.where(turn_of_lane == keep, moved, extra)
            outgoing = jnp.concatenate([outgoing, extra], axis=0)
        send_ref[...] = outgoing.T.reshape(peers, rows, width)[:, :kept]
        send_all(turn)

        far = dot(arrived_ref[...], spread_ref[:, asks:]).reshape(2, sites, sites, owned)
        current = part_ref[...] + far
        power_ref[before] = current
        high, low = split(current.reshape(2 * pairs, owned))
        halves_ref[...] = jnp.concatenate([high, low], axis=1)
        fetched_ref[...] = dot(halves_ref[...], select_ref[...]).reshape(2, sites, sites, wide)
        high = jnp.concatenate([halves_ref[:pairs, :owned], halves_ref[pairs:, :owned]], axis=1)
        low = jnp.concatenate([halves_ref[:pairs, owned:], halves_ref[pairs:, owned:]], axis=1)
        both = dot(super_ref[...], high)
        bracket = both[:pairs] + both[pairs:] + dot(super_ref[:pairs], low)
        part_ref[0] = (
            bracket[:, owned:].reshape(sites, sites, owned) - decay * power_ref[before, 0]
        )
        part_ref[1] = (
            -bracket[:, :owned].reshape(sites, sites, owned) - decay * power_ref[before, 1]
        )

        def near(row, carry):
            real, imag = part_ref[0, row], part_ref[1, row]
            for link in range(links):
                lanes = slice(link * owned, (link + 1) * owned)
                weight_real, weight_imag = (weight_ref[k, row, :, lanes] for k in range(2))
                source_real, source_imag = (fetched_ref[k, row, :, lanes] for k in range(2))
                real = real + (weight_real * source_imag + weight_imag * source_real)
                imag = imag + (weight_imag * source_imag - weight_real * source_real)
            part_ref[0, row] = real
            part_ref[1, row] = imag
            return carry

        lax.fori_loop(0, sites, near, 0)
        prepare()

        wait_all(turn)
        full_ref[:, :kept] = recv_ref[turn - 1]
        found = full_ref[...].reshape(asks, width).T
        if spare:
            extra = found[4 * sites :]
            parts = [found[k : k + spare] for k in range(0, 4 * sites, spare)]
            for keep, drop, piece in moves:
                moved = pltpu.roll(extra, drop - keep, 1)
                parts[piece] = jnp.where(turn_of_lane == drop, moved, parts[piece])
            found = jnp.concatenate(parts, axis=0)
        row_real, row_imag = found[:sites], found[sites : 2 * sites]
        col_real, col_imag = found[2 * sites : 3 * sites], found[3 * sites : 4 * sites]
        tl = (
            left_real * row_imag + left_imag * row_real,
            left_imag * row_imag - left_real * row_real,
        )
        tr_ref[0] = -(right_real * col_imag + right_imag * col_real)
        tr_ref[1] = right_real * col_real - right_imag * col_imag
        own_col = own_col_ref[...]
        blocks = [
            tl[part] * own_row_ref[row] + own_col * tr_ref[part, row : row + 1, :]
            for part in range(2)
            for row in range(sites)
        ]
        high, low = split(jnp.concatenate(blocks, axis=0))
        arrived_ref[...] = jnp.concatenate([high, low], axis=1)
        return carry

    turns = len(ERRORS)
    lax.fori_loop(1, turns + 1, advance, 0)
    far = dot(arrived_ref[...], spread_ref[:, asks:]).reshape(2, sites, sites, owned)
    power_ref[turns] = part_ref[...] + far

    def combine(poly):
        terms = [
            power_ref[k] if c == 1.0 else power_ref[k] * c for k, c in enumerate(poly) if c != 0.0
        ]
        return functools.reduce(jnp.add, terms)

    increment = combine([0.0] + NEW_POLY[1:])
    out_ref[...] = increment
    new_state = power_ref[0] + increment
    scale = ABS_TOL + REL_TOL * jnp.maximum(jnp.abs(power_ref[0]), jnp.abs(new_state))
    ratio = combine(ERR_POLY) / scale
    tile = jnp.sum((ratio * ratio).reshape(2 * pairs // 8, 8, owned), axis=0)
    tile = jnp.sum(tile, axis=0, keepdims=True)
    tile = jnp.sum(tile, axis=1, keepdims=True)
    note_ref[1] = jnp.broadcast_to(tile[None], (peers, 1, 128))
    send_note(1)
    wait_note(1)
    total = jnp.sum(noted_ref[1], axis=0)
    entries = 2 * pairs * owned * peers
    norm_ref[...] = jnp.sqrt(total[:, :1] / entries)


def shards(
    state, hamiltonian, mode_rates, ado_modes, link_src, link_site, link_coef, send_ids, step_units
):
    groups = lax.axis_size("grp")
    members = lax.axis_size("dev")
    sites, owned = state.shape[1], state.shape[3]
    links = link_src.shape[0]
    received = send_ids.shape[1]
    asks = received * USES
    wide = links * owned
    pairs = sites * sites
    width = -(-4 * sites // 128) * 128
    peers = groups * members
    rows = asks // peers
    kept, _, _ = folding(rows, 4 * sites, width)
    turns = len(ERRORS)
    vmem = pl.BlockSpec(memory_space=pltpu.VMEM)
    hbm = pl.BlockSpec(memory_space=pltpu.HBM)
    increment, norm = pl.pallas_call(
        functools.partial(kernel, groups, members),
        out_shape=(
            jax.ShapeDtypeStruct(state.shape, F32),
            jax.ShapeDtypeStruct((1, 1), F32),
        ),
        in_specs=[hbm] * 9,
        out_specs=(vmem, vmem),
        scratch_shapes=[
            pltpu.VMEM(hamiltonian.shape, F32),
            pltpu.VMEM((1, mode_rates.shape[0]), F32),
            pltpu.VMEM(ado_modes.shape, jnp.int32),
            pltpu.VMEM(link_src.shape, jnp.int32),
            pltpu.VMEM(link_site.shape, jnp.int32),
            pltpu.VMEM(link_coef.shape, F32),
            pltpu.VMEM(send_ids.shape, jnp.int32),
            pltpu.SMEM((1, 1), jnp.int32),
            pltpu.VMEM((len(ERRORS) + 1,) + state.shape, F32),
            pltpu.VMEM(state.shape, F32),
            pltpu.VMEM((2 * pairs, pairs), BF16),
            pltpu.VMEM((2 * owned, asks), BF16),
            pltpu.VMEM((2 * owned, wide), BF16),
            pltpu.VMEM((asks, wide), F32),
            pltpu.VMEM((2 * asks, asks + owned), BF16),
            pltpu.VMEM((2, sites, sites, wide), F32),
            pltpu.VMEM((sites, 1, asks), F32),
            pltpu.VMEM((sites, asks), F32),
            pltpu.VMEM((sites, 1, asks), F32),
            pltpu.VMEM((sites, asks), F32),
            pltpu.VMEM((2, sites, sites, asks), F32),
            pltpu.VMEM((2, sites, asks), F32),
            pltpu.VMEM((2 * pairs, 2 * owned), BF16),
            pltpu.VMEM((2 * pairs, 2 * asks), BF16),
            pltpu.VMEM((2, sites, sites, wide), F32),
            pltpu.VMEM((2, sites, asks), F32),
            pltpu.VMEM((peers, kept, width), F32),
            pltpu.VMEM((peers, rows, width), F32),
            pltpu.VMEM((turns, peers, kept, width), F32),
            pltpu.VMEM((2, peers, 1, 128), F32),
            pltpu.VMEM((2, peers, 1, 128), F32),
            pltpu.SemaphoreType.DMA((9,)),
            pltpu.SemaphoreType.DMA((turns,)),
            pltpu.SemaphoreType.DMA((turns,)),
            pltpu.SemaphoreType.DMA((2,)),
            pltpu.SemaphoreType.DMA((2,)),
        ],
        compiler_params=pltpu.CompilerParams(
            collective_id=0, has_side_effects=True, vmem_limit_bytes=64 * 1024 * 1024
        ),
    )(
        state,
        hamiltonian,
        mode_rates.reshape(1, -1),
        ado_modes,
        link_src,
        link_site,
        link_coef,
        send_ids,
        step_units.reshape(1, 1),
    )
    return state + increment, norm.reshape(())


def solution(mesh):
    return jax.shard_map(
        shards,
        mesh=mesh,
        in_specs=(
            P(None, None, None, ("grp", "dev")),
            P(),
            P(),
            P(None, ("grp", "dev")),
            P(None, ("grp", "dev")),
            P(None, ("grp", "dev")),
            P(None, None, ("grp", "dev")),
            P(("grp", "dev"), None),
            P(),
        ),
        out_specs=(P(None, None, None, ("grp", "dev")), P()),
        check_vma=False,
    )
```
